256 devices in a mesh: wide: 128 (over x, y_hi, z, core), narrow: 2 (over y_lo).
Axes of the slice: x: 4, y: 4 (y_hi: 2, y_lo: 2; y = y_hi * 2 + y_lo), z: 8, core: 2. Of those that a mesh axis runs over, the one named last changes fastest.
Arguments:
- functions: bfloat16 [1024, 65536], P(('wide', 'narrow')), may hold values from -6 to 6
- potential: float32 [64, 1024], replicated, may hold values from 0 to 2
- cheb_coef: float32 [9], replicated, may hold values from -1 to 1
- block_cols: int32 [16, 12], replicated, may hold values from 0 to 15, all different within a row
- kernel_halves: bfloat16 [2, 16, 12, 2048], P('narrow'), may hold values from -0.21875 to 0.21875
Outputs:
- updated_functions: bfloat16 [1024, 65536], P(('wide', 'narrow'))
The draws below stay inside these ranges and needn't reach their ends.
Inputs may be any that keep to these rules, and one draw needn't show every extreme that they name: `block_cols`: each block row names 12 different column blocks, and every column block is named by some block row.
All inputs are finite; a program needn't handle non-finite values.
Results may differ from the reference program's by a relative error of at most 0.0071.
Values may be sent and summed in bfloat16 or wider, within the bound.
No kernel may reach another device: no remote copies, remote signals or barrier semaphores. Data moves between devices by JAX's collectives and lax.ppermute only.
A program may use at most 64 MiB of HBM per device.

```python
import jax
import jax.numpy as jnp
from jax import lax

FUN_DEV = 4
BOX_X = 64
BOX_Y = 32
BOX_Z = 32
BLOCK = 64
DEGREE = 8
UPDATES = 2
GRID = 65536
FUNCS = 1024
ROW_BLOCKS = 16
SLOTS = 12


def levels(key, shape, shards, smallest, largest):
    def one(dim, shards_of):
        steps = jax.random.uniform(jax.random.fold_in(jax.random.fold_in(key, 6), dim), (shards_of,), jnp.float32, smallest / len(shards), largest / len(shards))
        return jnp.repeat(jnp.exp(steps), shape[dim] // shards_of).reshape((-1,) + (1,) * (len(shape) - dim - 1))

    level = one(*shards[0])
    for cut in shards[1:]:
        level = level * one(*cut)
    return level


def distinct(own_key, rows, amount, top, lift):
    ranking = jax.random.permutation(jax.random.fold_in(own_key, 1), amount)
    boost = ranking
    for power in range(3):
        boost = boost * boost // amount
    boost = boost * lift // amount
    tickets = jax.random.randint(jax.random.fold_in(own_key, 2), (rows, amount), 0, 4096) + boost
    holders = jax.random.permutation(jax.random.fold_in(own_key, 3), rows)[jnp.arange(amount) % rows]
    tickets = jnp.where(jnp.arange(rows)[:, None] == holders[None, :], 1 << 14, tickets)
    score = tickets * amount + jnp.arange(amount)
    return lax.top_k(score.astype(jnp.int32), top)[1].astype(jnp.int32)


def centred(key, shape, width, most, cuts=(), kind=jnp.bfloat16):
    values = width * jax.random.normal(key, shape, jnp.float32)
    if cuts:
        values = values * levels(key, shape, cuts, -0.22, 0.18)
    return jnp.clip(values, -most, most).astype(kind)


def setup_inputs(seed: int = 0) -> dict:
    key_of = jax.random.split(jax.random.key(seed), 6)
    functions = centred(key_of[0], (FUNCS, GRID), 1.0, 6.0, ((0, 256),))
    potential = jnp.clip(jax.random.uniform(key_of[1], (BOX_X, BOX_Y * BOX_Z), jnp.float32, 0.0, 2.0), 0.0, 2.0)
    cheb_coef = centred(key_of[2], (DEGREE + 1,), 0.4, 1.0, (), jnp.float32)
    block_cols = distinct(key_of[3], ROW_BLOCKS, ROW_BLOCKS, SLOTS, 0)
    kernel_halves = centred(key_of[4], (2, ROW_BLOCKS, SLOTS, BLOCK * BLOCK // 2), (SLOTS * BLOCK) ** -0.5, 0.21875, ((0, 2),))
    return dict(functions=functions, potential=potential, cheb_coef=cheb_coef, block_cols=block_cols, kernel_halves=kernel_halves)


def neighbour_sum(field):
    plane = BOX_Y * BOX_Z
    xpad = jnp.pad(field, ((0, 0), (1, 1), (0, 0)))
    neighbours = xpad[:, 2:, :] + xpad[:, :-2, :]
    ypad = jnp.pad(field, ((0, 0), (0, 0), (BOX_Z, BOX_Z)))
    neighbours = neighbours + ypad[:, :, 2 * BOX_Z:] + ypad[:, :, :plane]
    zpad = jnp.pad(field, ((0, 0), (0, 0), (1, 1)))
    position = jnp.arange(plane) % BOX_Z
    above_cell = jnp.where(position < BOX_Z - 1, zpad[:, :, 2:], 0.0)
    below_cell = jnp.where(position > 0, zpad[:, :, :plane], 0.0)
    return neighbours + above_cell + below_cell


def hamiltonian(field, shifted):
    return (shifted * field - 0.5 * neighbour_sum(field)) * 0.25


def chebyshev(function_rows, shifted, coefficient):
    row_count = function_rows.shape[0]
    field = function_rows.astype(jnp.float32).reshape(row_count, BOX_X, BOX_Y * BOX_Z)
    nearer = coefficient[DEGREE] * field
    farther = jnp.zeros_like(field)
    for order in range(DEGREE - 1, 0, -1):
        newest = coefficient[order] * field + 2.0 * hamiltonian(nearer, shifted) - farther
        farther = nearer
        nearer = newest
    result = coefficient[0] * field + hamiltonian(nearer, shifted) - farther
    return result.reshape(row_count, GRID).astype(jnp.bfloat16)


def reference(functions, potential, cheb_coef, block_cols, kernel_halves):
    shifted = potential - 1.0
    current = functions
    for update in range(UPDATES):
        filtered = lax.map(lambda rows: chebyshev(rows, shifted, cheb_coef),
                           current.reshape(FUNCS // BLOCK, BLOCK, GRID)).reshape(FUNCS, GRID)
        grouped = filtered.reshape(FUNCS // (2 * FUN_DEV), 2, FUN_DEV, GRID)
        source_sides = jnp.stack([grouped[:, 0].reshape(ROW_BLOCKS, BLOCK // 2, GRID),
                                  grouped[:, 1].reshape(ROW_BLOCKS, BLOCK // 2, GRID)])

        def row_block(row_index):
            summed = jnp.zeros((BLOCK, GRID), jnp.float32)
            for half_index in range(2):
                picked = source_sides[half_index][block_cols[row_index]]
                kernel_rows = kernel_halves[half_index, row_index].reshape(SLOTS, BLOCK, BLOCK // 2)
                kernel_rows = kernel_rows.transpose(1, 0, 2).reshape(BLOCK, SLOTS * (BLOCK // 2))
                product = jnp.dot(kernel_rows.astype(jnp.float32),
                                  picked.reshape(SLOTS * (BLOCK // 2), GRID).astype(jnp.float32),
                                  preferred_element_type=jnp.float32)
                rounded = lax.optimization_barrier(product.astype(jnp.bfloat16)).astype(jnp.float32)
                summed = summed + rounded
            return summed.astype(jnp.bfloat16)

        current = lax.map(row_block, jnp.arange(ROW_BLOCKS, dtype=jnp.int32)).reshape(FUNCS, GRID)
    return current
```

```python
import functools

import jax
import jax.numpy as jnp
from jax import lax
from jax.experimental import pallas as pl
from jax.experimental.pallas import tpu as pltpu
from jax.sharding import PartitionSpec as P

FUN_DEV = 4
BOX_X = 64
PLANE = 1024
BLOCK = 64
DEGREE = 8
UPDATES = 2
GRID = 65536
FUNCS = 1024
LANES = 128
SUBLANES = 8
X_IN = BOX_X // SUBLANES
Y_OUT = PLANE // LANES
TILES = GRID // LANES


def filter_kernel(coef_ref, potential_ref, in_ref, out_ref, wide_ref, plane_ref, shift_ref, field_ref, even_ref, odd_ref):
    lane = lax.broadcasted_iota(jnp.int32, (SUBLANES, LANES), 1)
    row = lax.broadcasted_iota(jnp.int32, (SUBLANES, LANES), 0)
    z = lane % 32
    wide_ref[...] = in_ref[...].astype(jnp.float32)
    for yo in range(Y_OUT):
        plane_ref[yo * BOX_X:(yo + 1) * BOX_X, :] = potential_ref[:, yo * LANES:(yo + 1) * LANES]
    for xi in range(X_IN):
        for yo in range(Y_OUT):
            potential = plane_ref[pl.ds(yo * BOX_X + xi, SUBLANES, stride=X_IN), :]
            shift_ref[xi, yo] = 0.5 * (potential - 1.0)

    def stencil_step(source, target, coefficient, last, first):
        zero = jnp.zeros((SUBLANES, LANES), jnp.float32)
        for xi in range(X_IN):
            line = [source[xi, yo] for yo in range(Y_OUT)]
            up = [pltpu.roll(v, 96, 1) for v in line] + [zero]
            down = [zero] + [pltpu.roll(v, 32, 1) for v in line]
            for yo in range(Y_OUT):
                v = line[yo]
                if xi < X_IN - 1:
                    right = source[xi + 1, yo]
                else:
                    right = jnp.where(row < SUBLANES - 1, pltpu.roll(source[0, yo], SUBLANES - 1, 0), 0.0)
                if xi > 0:
                    left = source[xi - 1, yo]
                else:
                    left = jnp.where(row > 0, pltpu.roll(source[X_IN - 1, yo], 1, 0), 0.0)
                total = left + right
                total = total + jnp.where(lane < 96, up[yo], up[yo + 1])
                total = total + jnp.where(lane >= 32, down[yo + 1], down[yo])
                total = total + jnp.where(z < 31, pltpu.roll(v, 127, 1), 0.0)
                total = total + jnp.where(z > 0, pltpu.roll(v, 1, 1), 0.0)
                applied = shift_ref[xi, yo] * v - 0.25 * total
                if last:
                    applied = 0.5 * applied
                value = coefficient * field_ref[xi, yo] + applied
                if not first:
                    value = value - target[xi, yo]
                target[xi, yo] = value

    def one_function(fun, carry):
        for xi in range(X_IN):
            for yo in range(Y_OUT):
                start = (xi * Y_OUT + yo) * FUN_DEV + fun
                field_ref[xi, yo] = wide_ref[pl.ds(start, SUBLANES, stride=X_IN * Y_OUT * FUN_DEV), :]

        def one_update(update, carry):
            for xi in range(X_IN):
                for yo in range(Y_OUT):
                    even_ref[xi, yo] = coef_ref[DEGREE] * field_ref[xi, yo]
            source, target = even_ref, odd_ref
            for order in range(DEGREE - 1, -1, -1):
                stencil_step(source, target, coef_ref[order], order == 0, order == DEGREE - 1)
                source, target = target, source
            for xi in range(X_IN):
                for yo in range(Y_OUT):
                    field_ref[xi, yo] = source[xi, yo]
            return carry

        lax.fori_loop(0, UPDATES, one_update, 0)
        for xi in range(X_IN):
            for yo in range(Y_OUT):
                start = (xi * Y_OUT + yo) * FUN_DEV + fun
                wide_ref[pl.ds(start, SUBLANES, stride=X_IN * Y_OUT * FUN_DEV), :] = field_ref[xi, yo]
        return carry

    lax.fori_loop(0, FUN_DEV, one_function, 0)
    out_ref[...] = wide_ref[...].astype(jnp.bfloat16)


def filter_twice(rows, potential, coefficient):
    vectors = pltpu.VMEM((X_IN, Y_OUT, SUBLANES, LANES), jnp.float32)
    return pl.pallas_call(
        filter_kernel,
        name="filter_twice",
        out_shape=jax.ShapeDtypeStruct(rows.shape, jnp.bfloat16),
        in_specs=[
            pl.BlockSpec(memory_space=pltpu.SMEM),
            pl.BlockSpec(memory_space=pltpu.VMEM),
            pl.BlockSpec(memory_space=pltpu.VMEM),
        ],
        out_specs=pl.BlockSpec(memory_space=pltpu.VMEM),
        scratch_shapes=[pltpu.VMEM(rows.shape, jnp.float32), pltpu.VMEM((BOX_X * Y_OUT, LANES), jnp.float32), vectors, vectors, vectors, vectors],
        compiler_params=pltpu.CompilerParams(vmem_limit_bytes=16 * 2**20),
        cost_estimate=pl.CostEstimate(flops=60_000_000, bytes_accessed=40_000_000, transcendentals=0),
    )(coefficient, potential, rows)


def mix_kernel(mixer_ref, points_ref, out_ref, middle_ref):
    middle_ref[...] = jnp.dot(
        mixer_ref[...], points_ref[...], preferred_element_type=jnp.float32
    ).astype(jnp.bfloat16)
    out_ref[...] = jnp.dot(
        mixer_ref[...], middle_ref[...], preferred_element_type=jnp.float32
    ).astype(jnp.bfloat16)


def mix_twice(mixer, points):
    return pl.pallas_call(
        mix_kernel,
        name="mix_twice",
        out_shape=jax.ShapeDtypeStruct(points.shape, jnp.bfloat16),
        in_specs=[pl.BlockSpec(memory_space=pltpu.VMEM)] * 2,
        out_specs=pl.BlockSpec(memory_space=pltpu.VMEM),
        scratch_shapes=[pltpu.VMEM(points.shape, jnp.bfloat16)],
        compiler_params=pltpu.CompilerParams(vmem_limit_bytes=24 * 2**20),
        cost_estimate=pl.CostEstimate(flops=1_100_000_000, bytes_accessed=4_000_000, transcendentals=0),
    )(mixer, points)


def dense_mixer(halves, block_cols):
    row_blocks, slots = block_cols.shape
    chosen = (block_cols[:, :, None] == jnp.arange(row_blocks)[None, None, :]).astype(jnp.bfloat16)
    spread = jnp.einsum("rsb,prsk->prbk", chosen, halves, preferred_element_type=jnp.float32).astype(jnp.bfloat16)
    spread = spread.reshape(2, row_blocks, row_blocks, BLOCK // (2 * FUN_DEV), 2, FUN_DEV, BLOCK // 2)
    return spread.transpose(4, 1, 3, 5, 0, 2, 6).reshape(FUNCS, FUNCS)


def local(functions, potential, cheb_coef, block_cols, kernel_halves):
    devices = lax.axis_size("wide") * lax.axis_size("narrow")
    own = GRID // devices
    halves = lax.all_gather(kernel_halves, "narrow", axis=0, tiled=True)
    mixer = dense_mixer(halves, block_cols)
    rows = functions.reshape(FUN_DEV, TILES, LANES).transpose(1, 0, 2).reshape(TILES * FUN_DEV, LANES)
    filtered = filter_twice(rows, potential, cheb_coef)
    outgoing = filtered.reshape(devices, own // LANES, FUN_DEV, LANES).transpose(0, 2, 1, 3)
    outgoing = outgoing.reshape(devices, FUN_DEV, own)
    points = lax.all_to_all(outgoing, ("narrow", "wide"), split_axis=0, concat_axis=0, tiled=True)
    mixed = mix_twice(mixer, points.reshape(FUNCS, own))
    result = lax.all_to_all(
        mixed.reshape(devices, FUN_DEV, own), ("narrow", "wide"), split_axis=0, concat_axis=0, tiled=True
    )
    return result.transpose(1, 0, 2).reshape(FUN_DEV, GRID)


def solution(mesh):
    return jax.shard_map(
        local,
        mesh=mesh,
        in_specs=(P(("wide", "narrow"), None), P(), P(), P(), P("narrow", None, None, None)),
        out_specs=P(("wide", "narrow"), None),
        check_vma=False,
    )
```

```python
import jax
import jax.numpy as jnp
from jax import lax
from jax.experimental import pallas as pl
from jax.experimental.pallas import tpu as pltpu
from jax.sharding import PartitionSpec as P

FUN_DEV = 4
BOX_X = 64
BOX_Y = 32
BOX_Z = 32
BLOCK = 64
DEGREE = 8
UPDATES = 2
GRID = 65536
FUNCS = 1024
LANES = 128
SUBLANES = 8
X_IN = BOX_X // SUBLANES
Y_OUT = BOX_Y * BOX_Z // LANES
TILES = GRID // LANES


def swap_chunks(group, lane):
    low = lane < 64
    even = (lane // 32) % 2 == 0
    upper, lower = [], []
    for first, second in ((group[0], group[2]), (group[1], group[3])):
        upper.append(jnp.where(low, first, pltpu.roll(second, 64, 1)))
        lower.append(jnp.where(low, pltpu.roll(first, 64, 1), second))
    out = []
    for first, second in (upper, lower):
        out.append(jnp.where(even, first, pltpu.roll(second, 32, 1)))
        out.append(jnp.where(even, pltpu.roll(first, 96, 1), second))
    return out


def filter_kernel(coef_ref, potential_ref, in_ref, out_ref, wide_ref, plane_ref, shift_ref, field_ref, even_ref, odd_ref):
    lane = lax.broadcasted_iota(jnp.int32, (SUBLANES, LANES), 1)
    row = lax.broadcasted_iota(jnp.int32, (SUBLANES, LANES), 0)
    z = lane % 32
    wide_ref[...] = in_ref[...].astype(jnp.float32)
    for yo in range(Y_OUT):
        plane_ref[yo * BOX_X:(yo + 1) * BOX_X, :] = potential_ref[:, yo * LANES:(yo + 1) * LANES]
    for xi in range(X_IN):
        for yo in range(Y_OUT):
            potential = plane_ref[pl.ds(yo * BOX_X + xi, SUBLANES, stride=X_IN), :]
            shift_ref[xi, yo] = 0.5 * (potential - 1.0)

    def stencil_step(source, target, coefficient, last, first):
        zero = jnp.zeros((SUBLANES, LANES), jnp.float32)
        for xi in range(X_IN):
            line = [source[xi, yo] for yo in range(Y_OUT)]
            up = [pltpu.roll(v, 96, 1) for v in line] + [zero]
            down = [zero] + [pltpu.roll(v, 32, 1) for v in line]
            for yo in range(Y_OUT):
                v = line[yo]
                if xi < X_IN - 1:
                    right = source[xi + 1, yo]
                else:
                    right = jnp.where(row < SUBLANES - 1, pltpu.roll(source[0, yo], SUBLANES - 1, 0), 0.0)
                if xi > 0:
                    left = source[xi - 1, yo]
                else:
                    left = jnp.where(row > 0, pltpu.roll(source[X_IN - 1, yo], 1, 0), 0.0)
                total = left + right
                total = total + jnp.where(lane < 96, up[yo], up[yo + 1])
                total = total + jnp.where(lane >= 32, down[yo + 1], down[yo])
                total = total + jnp.where(z < 31, pltpu.roll(v, 127, 1), 0.0)
                total = total + jnp.where(z > 0, pltpu.roll(v, 1, 1), 0.0)
                applied = shift_ref[xi, yo] * v - 0.25 * total
                if last:
                    applied = 0.5 * applied
                value = coefficient * field_ref[xi, yo] + applied
                if not first:
                    value = value - target[xi, yo]
                target[xi, yo] = value

    def one_function(fun, carry):
        for xi in range(X_IN):
            for yo in range(Y_OUT):
                start = (xi * Y_OUT + yo) * FUN_DEV + fun
                field_ref[xi, yo] = wide_ref[pl.ds(start, SUBLANES, stride=X_IN * Y_OUT * FUN_DEV), :]

        def one_update(update, carry):
            for xi in range(X_IN):
                for yo in range(Y_OUT):
                    even_ref[xi, yo] = coef_ref[DEGREE] * field_ref[xi, yo]
            source, target = even_ref, odd_ref
            for order in range(DEGREE - 1, -1, -1):
                stencil_step(source, target, coef_ref[order], order == 0, order == DEGREE - 1)
                source, target = target, source
            for xi in range(X_IN):
                for yo in range(Y_OUT):
                    field_ref[xi, yo] = source[xi, yo]
            return carry

        lax.fori_loop(0, UPDATES, one_update, 0)
        for xi in range(X_IN):
            for yo in range(Y_OUT):
                start = (xi * Y_OUT + yo) * FUN_DEV + fun
                wide_ref[pl.ds(start, SUBLANES, stride=X_IN * Y_OUT * FUN_DEV), :] = field_ref[xi, yo]
        return carry

    lax.fori_loop(0, FUN_DEV, one_function, 0)
    out_ref[...] = wide_ref[...].astype(jnp.bfloat16)


def filter_twice(rows, potential, coefficient):
    vectors = pltpu.VMEM((X_IN, Y_OUT, SUBLANES, LANES), jnp.float32)
    return pl.pallas_call(
        filter_kernel,
        name="filter_twice",
        out_shape=jax.ShapeDtypeStruct(rows.shape, jnp.bfloat16),
        in_specs=[
            pl.BlockSpec(memory_space=pltpu.SMEM),
            pl.BlockSpec(memory_space=pltpu.VMEM),
            pl.BlockSpec(memory_space=pltpu.VMEM),
        ],
        out_specs=pl.BlockSpec(memory_space=pltpu.VMEM),
        scratch_shapes=[pltpu.VMEM(rows.shape, jnp.float32), pltpu.VMEM((BOX_X * Y_OUT, LANES), jnp.float32), vectors, vectors, vectors, vectors],
        compiler_params=pltpu.CompilerParams(vmem_limit_bytes=16 * 2**20),
        cost_estimate=pl.CostEstimate(flops=60_000_000, bytes_accessed=40_000_000, transcendentals=0),
    )(coefficient, potential, rows)


def mix_kernel(mixer_ref, points_ref, out_ref, middle_ref):
    middle_ref[...] = jnp.dot(
        mixer_ref[...], points_ref[...], preferred_element_type=jnp.float32
    ).astype(jnp.bfloat16)
    out_ref[...] = jnp.dot(
        mixer_ref[...], middle_ref[...], preferred_element_type=jnp.float32
    ).astype(jnp.bfloat16)


def mix_twice(mixer, points):
    return pl.pallas_call(
        mix_kernel,
        name="mix_twice",
        out_shape=jax.ShapeDtypeStruct(points.shape, jnp.bfloat16),
        in_specs=[pl.BlockSpec(memory_space=pltpu.VMEM)] * 2,
        out_specs=pl.BlockSpec(memory_space=pltpu.VMEM),
        scratch_shapes=[pltpu.VMEM(points.shape, jnp.bfloat16)],
        compiler_params=pltpu.CompilerParams(vmem_limit_bytes=24 * 2**20),
        cost_estimate=pl.CostEstimate(flops=1_100_000_000, bytes_accessed=4_000_000, transcendentals=0),
    )(mixer, points)


def spread_kernel(half_ref, place_ref, own_ref, other_ref, out_ref, wide_ref):
    lane = lax.broadcasted_iota(jnp.int32, (SUBLANES, LANES), 1)
    row_blocks = FUNCS // BLOCK
    column_tiles = FUNCS // 2 // LANES
    for source_ref, half in ((own_ref, half_ref[0]), (other_ref, 1 - half_ref[0])):
        def one_pair(pair, carry, source_ref=source_ref, half=half):
            spread = jnp.dot(
                place_ref[...],
                source_ref[:, pl.ds(pl.multiple_of(pair * 2 * LANES, 2 * LANES), 2 * LANES)],
                preferred_element_type=jnp.float32,
            )
            for side in range(2):
                for tile in range(column_tiles):
                    for rows in range(row_blocks // SUBLANES):
                        group = [
                            spread[
                                (tile * 4 + step) * row_blocks + rows * SUBLANES:
                                (tile * 4 + step) * row_blocks + (rows + 1) * SUBLANES,
                                side * LANES:(side + 1) * LANES,
                            ]
                            for step in range(4)
                        ]
                        for fun, value in enumerate(swap_chunks(group, lane)):
                            start = (half * column_tiles + tile) * FUNCS
                            start = start + side * (FUNCS // 2) + rows * SUBLANES * (BLOCK // 2) + pair * FUN_DEV + fun
                            wide_ref[pl.ds(start, SUBLANES, stride=BLOCK // 2), :] = value
            return carry

        lax.fori_loop(0, BLOCK * BLOCK // 2 // (2 * LANES), one_pair, 0)
    for tile in range(FUNCS // LANES):
        out_ref[:, tile * LANES:(tile + 1) * LANES] = wide_ref[tile * FUNCS:(tile + 1) * FUNCS, :].astype(jnp.bfloat16)


def dense_mixer(half, own, other, block_cols):
    row_blocks, slots = block_cols.shape
    entry = jnp.arange(slots * row_blocks)
    place = jnp.arange(row_blocks * row_blocks)
    column = block_cols.T.reshape(-1)
    chosen = (column[None, :] == place[:, None] // row_blocks) & (
        entry[None, :] % row_blocks == place[:, None] % row_blocks
    )

    def flat(blocks):
        return blocks[0].transpose(1, 0, 2).reshape(slots * row_blocks, BLOCK * BLOCK // 2)

    return pl.pallas_call(
        spread_kernel,
        name="spread_blocks",
        out_shape=jax.ShapeDtypeStruct((FUNCS, FUNCS), jnp.bfloat16),
        in_specs=[pl.BlockSpec(memory_space=pltpu.SMEM)] + [pl.BlockSpec(memory_space=pltpu.VMEM)] * 3,
        out_specs=pl.BlockSpec(memory_space=pltpu.VMEM),
        scratch_shapes=[pltpu.VMEM((FUNCS * FUNCS // LANES, LANES), jnp.float32)],
        compiler_params=pltpu.CompilerParams(vmem_limit_bytes=16 * 2**20),
        cost_estimate=pl.CostEstimate(flops=400_000_000, bytes_accessed=15_000_000, transcendentals=0),
    )(half.reshape(1), chosen.astype(jnp.bfloat16), flat(own), flat(other))


def other_half_pairs(wide, narrow):
    pairs = []
    for target in range(wide * narrow):
        rest, low = divmod(target, 2)
        rest, core = divmod(rest, 2)
        rest, z = divmod(rest, 8)
        x, high = divmod(rest, 2)
        y = (high * 2 + low + (1 if core == 0 else 3)) % 4
        pairs.append(((((x * 2 + y // 2) * 8 + z) * 2 + core) * 2 + y % 2, target))
    return pairs


def local(functions, potential, cheb_coef, block_cols, kernel_halves):
    devices = lax.axis_size("wide") * lax.axis_size("narrow")
    own = GRID // devices
    other = lax.ppermute(
        kernel_halves, ("wide", "narrow"), other_half_pairs(lax.axis_size("wide"), lax.axis_size("narrow"))
    )
    rows = functions.reshape(FUN_DEV, TILES, LANES).transpose(1, 0, 2).reshape(TILES * FUN_DEV, LANES)
    filtered = filter_twice(rows, potential, cheb_coef)
    filtered, other = lax.optimization_barrier((filtered, other))
    mixer = dense_mixer(lax.axis_index("narrow"), kernel_halves, other, block_cols)
    outgoing = filtered.reshape(devices, own // LANES, FUN_DEV, LANES).transpose(0, 2, 1, 3)
    outgoing = outgoing.reshape(devices, FUN_DEV, own)
    points = lax.all_to_all(outgoing, ("narrow", "wide"), split_axis=0, concat_axis=0, tiled=True)
    mixed = mix_twice(mixer, points.reshape(FUNCS, own))
    result = lax.all_to_all(
        mixed.reshape(devices, FUN_DEV, own), ("narrow", "wide"), split_axis=0, concat_axis=0, tiled=True
    )
    return result.transpose(1, 0, 2).reshape(FUN_DEV, GRID)


def solution(mesh):
    return jax.shard_map(
        local,
        mesh=mesh,
        in_specs=(P(("wide", "narrow"), None), P(), P(), P(), P("narrow", None, None, None)),
        out_specs=P(("wide", "narrow"), None),
        check_vma=False,
    )
```

```python
import jax
import jax.numpy as jnp
from jax import lax
from jax.experimental import pallas as pl
from jax.experimental.pallas import tpu as pltpu
from jax.sharding import PartitionSpec as P

FUN_DEV = 4
BOX_X = 64
BOX_Y = 32
BOX_Z = 32
BLOCK = 64
DEGREE = 8
UPDATES = 2
GRID = 65536
FUNCS = 1024
LANES = 128
SUBLANES = 8
X_FAR = 2
X_IN = 8
PARTS = 16
Y_OUT = BOX_Y * BOX_Z // LANES
TILES = GRID // LANES


def swap_chunks(group, lane):
    low = lane < 64
    even = (lane // 32) % 2 == 0
    upper, lower = [], []
    for first, second in ((group[0], group[2]), (group[1], group[3])):
        upper.append(jnp.where(low, first, pltpu.roll(second, 64, 1)))
        lower.append(jnp.where(low, pltpu.roll(first, 64, 1), second))
    out = []
    for first, second in (upper, lower):
        out.append(jnp.where(even, first, pltpu.roll(second, 32, 1)))
        out.append(jnp.where(even, pltpu.roll(first, 96, 1), second))
    return out


def point_order(size):
    first = lax.broadcasted_iota(jnp.int32, (size, size), 0)
    second = lax.broadcasted_iota(jnp.int32, (size, size), 1)
    column = first // 32 * 32 + first % 8 * 4 + first // 8 % 4
    return (second == column).astype(jnp.float32).astype(jnp.bfloat16)


def filter_kernel(
    coef_hbm,
    potential_hbm,
    in_hbm,
    out_ref,
    coef_ref,
    potential_ref,
    in_ref,
    plane_ref,
    turned_ref,
    shift_ref,
    field_ref,
    even_ref,
    odd_ref,
    semaphores,
):
    arrivals = [
        pltpu.make_async_copy(source, target, semaphores.at[index])
        for index, (source, target) in enumerate(
            ((potential_hbm, potential_ref), (in_hbm, in_ref), (coef_hbm, coef_ref))
        )
    ]
    for arrival in arrivals:
        arrival.start()
    lane = lax.broadcasted_iota(jnp.int32, (SUBLANES, LANES), 1)
    row = lax.broadcasted_iota(jnp.int32, (SUBLANES, LANES), 0)
    y_out = (lane // FUN_DEV) % Y_OUT
    order_z = point_order(LANES)
    first = lax.broadcasted_iota(jnp.int32, (LANES, LANES), 0)
    second = lax.broadcasted_iota(jnp.int32, (LANES, LANES), 1)
    unit = (first == second).astype(jnp.float32).astype(jnp.bfloat16)
    x_rows = Y_OUT * FUN_DEV

    arrivals[0].wait()
    for yo in range(Y_OUT):
        for xo in range(BOX_X // SUBLANES):
            shifted = 0.5 * (potential_ref[xo * SUBLANES:(xo + 1) * SUBLANES, yo * LANES:(yo + 1) * LANES] - 1.0)
            for fun in range(FUN_DEV):
                start = xo * SUBLANES * x_rows + yo * FUN_DEV + fun
                plane_ref[pl.ds(start, SUBLANES, stride=x_rows), :] = shifted

    def rows_of(far, xi, out):
        return pl.ds((far * 32 + out * X_IN + xi) * x_rows, x_rows)

    arrivals[1].wait()
    for xi in range(X_IN):
        blocks = [(far, out) for far in range(X_FAR) for out in range(4)]
        fields = jnp.concatenate([in_ref[rows_of(far, xi, out), :] for far, out in blocks], 0)
        fields = lax.dot_general(order_z, fields, (((1,), (1,)), ((), ())), preferred_element_type=jnp.float32)
        for far in range(X_FAR):
            field_ref[far, xi] = fields[:, far * LANES:(far + 1) * LANES].reshape(PARTS, SUBLANES, LANES)
            shifts = jnp.concatenate([plane_ref[rows_of(far, xi, out), :] for out in range(4)], 0)
            turned_ref[far] = shifts.T
            for part in range(PARTS):
                shift_ref[far, xi, part] = turned_ref[far, pl.ds(part // 4 * 32 + part % 4, SUBLANES, stride=4), :]

    def plane_step(before, at, after, target, coefficient, scale, last, start, far, xi):
        for part in range(PARTS):
            yi, zi = part // 4, part % 4
            total = before[part] + after[part]
            if zi < 3:
                total = total + at[part + 1]
            else:
                total = total + jnp.where(row < SUBLANES - 1, pltpu.roll(at[yi * 4], SUBLANES - 1, 0), 0.0)
            if zi > 0:
                total = total + at[part - 1]
            else:
                total = total + jnp.where(row > 0, pltpu.roll(at[yi * 4 + 3], 1, 0), 0.0)
            if yi < 3:
                total = total + at[part + 4]
            else:
                total = total + jnp.where(y_out < Y_OUT - 1, pltpu.roll(at[zi], LANES - FUN_DEV, 1), 0.0)
            if yi > 0:
                total = total + at[part - 4]
            else:
                total = total + jnp.where(y_out > 0, pltpu.roll(at[12 + zi], FUN_DEV, 1), 0.0)
            applied = shift_ref[far, xi, part] * at[part] - 0.25 * total
            if scale is not None:
                applied = scale * applied
            value = coefficient * field_ref[far, xi, part] + applied
            if not start:
                value = value - target[far, xi, part]
            if last:
                field_ref[far, xi, part] = value
            else:
                target[far, xi, part] = value

    def stencil_step(source, target, coefficient, scale=None, last=False, start=False):
        def plane(far, xi):
            return [source[far, xi, part] for part in range(PARTS)]

        def below(far):
            own = [pltpu.roll(v, 32, 1) for v in plane(far, X_IN - 1)]
            if far == 0:
                return [jnp.where(lane < 32, 0.0, v) for v in own]
            return [jnp.where(lane < 32, pltpu.roll(v, 32, 1), w) for v, w in zip(plane(0, X_IN - 1), own)]

        def above(far):
            own = [pltpu.roll(v, 96, 1) for v in plane(far, 0)]
            if far == 1:
                return [jnp.where(lane >= 96, 0.0, v) for v in own]
            return [jnp.where(lane >= 96, pltpu.roll(v, 96, 1), w) for v, w in zip(plane(1, 0), own)]

        for far in range(X_FAR):
            before, at = below(far), plane(far, 0)
            for xi in range(X_IN):
                after = plane(far, xi + 1) if xi < X_IN - 1 else above(far)
                plane_step(before, at, after, target, coefficient, scale, last, start, far, xi)
                before, at = at, after

    def one_update(update, carry):
        stencil_step(field_ref, odd_ref, coef_ref[DEGREE - 1], scale=coef_ref[DEGREE], start=True)
        stencil_step(odd_ref, even_ref, coef_ref[DEGREE - 2] - coef_ref[DEGREE], start=True)

        def two_orders(pair, carry):
            order = DEGREE - 3 - 2 * pair
            stencil_step(even_ref, odd_ref, coef_ref[order])
            stencil_step(odd_ref, even_ref, coef_ref[order - 1])
            return carry

        lax.fori_loop(0, DEGREE // 2 - 2, two_orders, 0)
        stencil_step(even_ref, odd_ref, coef_ref[1])
        stencil_step(odd_ref, even_ref, coef_ref[0], scale=0.5, last=True)
        return carry

    arrivals[2].wait()
    lax.fori_loop(0, UPDATES, one_update, 0)

    for xi in range(X_IN):
        fields = field_ref[:, xi].reshape(X_FAR * LANES, LANES).astype(jnp.bfloat16)
        fields = lax.dot_general(unit, fields, (((1,), (1,)), ((), ())), preferred_element_type=jnp.float32)
        fields = fields.astype(jnp.bfloat16)
        for far in range(X_FAR):
            for out in range(4):
                rows = fields[out * x_rows:(out + 1) * x_rows, far * LANES:(far + 1) * LANES]
                out_ref[rows_of(far, xi, out), :] = rows


def filter_twice(rows, potential, coefficient):
    vectors = pltpu.VMEM((X_FAR, X_IN, PARTS, SUBLANES, LANES), jnp.float32)
    return pl.pallas_call(
        filter_kernel,
        name="filter_twice",
        out_shape=jax.ShapeDtypeStruct(rows.shape, jnp.bfloat16),
        in_specs=[pl.BlockSpec(memory_space=pltpu.HBM)] * 3,
        out_specs=pl.BlockSpec(memory_space=pltpu.VMEM),
        scratch_shapes=[
            pltpu.SMEM(coefficient.shape, jnp.float32),
            pltpu.VMEM(potential.shape, jnp.float32),
            pltpu.VMEM(rows.shape, jnp.bfloat16),
            pltpu.VMEM(rows.shape, jnp.float32),
            pltpu.VMEM((X_FAR, LANES, LANES), jnp.float32),
            vectors,
            vectors,
            vectors,
            vectors,
            pltpu.SemaphoreType.DMA((3,)),
        ],
        compiler_params=pltpu.CompilerParams(vmem_limit_bytes=60 * 2**20),
        cost_estimate=pl.CostEstimate(flops=60_000_000, bytes_accessed=40_000_000, transcendentals=0),
    )(coefficient, potential, rows)


def mix_kernel(mixer_ref, points_ref, out_ref, middle_ref):
    points = jnp.dot(points_ref[...], point_order(points_ref.shape[1]), preferred_element_type=jnp.float32)
    middle_ref[...] = jnp.dot(
        mixer_ref[...], points.astype(jnp.bfloat16), preferred_element_type=jnp.float32
    ).astype(jnp.bfloat16)
    out_ref[...] = jnp.dot(
        mixer_ref[...], middle_ref[...], preferred_element_type=jnp.float32
    ).astype(jnp.bfloat16)


def mix_twice(mixer, points):
    return pl.pallas_call(
        mix_kernel,
        name="mix_twice",
        out_shape=jax.ShapeDtypeStruct(points.shape, jnp.bfloat16),
        in_specs=[pl.BlockSpec(memory_space=pltpu.VMEM)] * 2,
        out_specs=pl.BlockSpec(memory_space=pltpu.VMEM),
        scratch_shapes=[pltpu.VMEM(points.shape, jnp.bfloat16)],
        compiler_params=pltpu.CompilerParams(vmem_limit_bytes=24 * 2**20),
        cost_estimate=pl.CostEstimate(flops=1_100_000_000, bytes_accessed=4_000_000, transcendentals=0),
    )(mixer, points)


def spread_kernel(half_ref, place_ref, own_ref, other_ref, out_ref, wide_ref):
    lane = lax.broadcasted_iota(jnp.int32, (SUBLANES, LANES), 1)
    row_blocks = FUNCS // BLOCK
    column_tiles = FUNCS // 2 // LANES
    for source_ref, half in ((own_ref, half_ref[0]), (other_ref, 1 - half_ref[0])):
        def one_pair(pair, carry, source_ref=source_ref, half=half):
            spread = jnp.dot(
                place_ref[...],
                source_ref[:, pl.ds(pl.multiple_of(pair * 2 * LANES, 2 * LANES), 2 * LANES)],
                preferred_element_type=jnp.float32,
            )
            for side in range(2):
                for tile in range(column_tiles):
                    for rows in range(row_blocks // SUBLANES):
                        group = [
                            spread[
                                (tile * 4 + step) * row_blocks + rows * SUBLANES:
                                (tile * 4 + step) * row_blocks + (rows + 1) * SUBLANES,
                                side * LANES:(side + 1) * LANES,
                            ]
                            for step in range(4)
                        ]
                        for fun, value in enumerate(swap_chunks(group, lane)):
                            start = (half * column_tiles + tile) * FUNCS
                            start = start + side * (FUNCS // 2) + rows * SUBLANES * (BLOCK // 2) + pair * FUN_DEV + fun
                            wide_ref[pl.ds(start, SUBLANES, stride=BLOCK // 2), :] = value
            return carry

        lax.fori_loop(0, BLOCK * BLOCK // 2 // (2 * LANES), one_pair, 0)
    for tile in range(FUNCS // LANES):
        out_ref[:, tile * LANES:(tile + 1) * LANES] = wide_ref[tile * FUNCS:(tile + 1) * FUNCS, :].astype(jnp.bfloat16)


def dense_mixer(half, own, other, block_cols):
    row_blocks, slots = block_cols.shape
    entry = jnp.arange(slots * row_blocks)
    place = jnp.arange(row_blocks * row_blocks)
    column = block_cols.T.reshape(-1)
    chosen = (column[None, :] == place[:, None] // row_blocks) & (
        entry[None, :] % row_blocks == place[:, None] % row_blocks
    )

    def flat(blocks):
        return blocks[0].transpose(1, 0, 2).reshape(slots * row_blocks, BLOCK * BLOCK // 2)

    return pl.pallas_call(
        spread_kernel,
        name="spread_blocks",
        out_shape=jax.ShapeDtypeStruct((FUNCS, FUNCS), jnp.bfloat16),
        in_specs=[pl.BlockSpec(memory_space=pltpu.SMEM)] + [pl.BlockSpec(memory_space=pltpu.VMEM)] * 3,
        out_specs=pl.BlockSpec(memory_space=pltpu.VMEM),
        scratch_shapes=[pltpu.VMEM((FUNCS * FUNCS // LANES, LANES), jnp.float32)],
        compiler_params=pltpu.CompilerParams(vmem_limit_bytes=16 * 2**20),
        cost_estimate=pl.CostEstimate(flops=400_000_000, bytes_accessed=15_000_000, transcendentals=0),
    )(half.reshape(1), chosen.astype(jnp.bfloat16), flat(own), flat(other))


def other_half_pairs(wide, narrow):
    pairs = []
    for target in range(wide * narrow):
        rest, low = divmod(target, 2)
        rest, core = divmod(rest, 2)
        rest, z = divmod(rest, 8)
        x, high = divmod(rest, 2)
        y = (high * 2 + low + (1 if core == 0 else 3)) % 4
        pairs.append(((((x * 2 + y // 2) * 8 + z) * 2 + core) * 2 + y % 2, target))
    return pairs


def local(functions, potential, cheb_coef, block_cols, kernel_halves):
    devices = lax.axis_size("wide") * lax.axis_size("narrow")
    own = GRID // devices
    other = lax.ppermute(
        kernel_halves, ("wide", "narrow"), other_half_pairs(lax.axis_size("wide"), lax.axis_size("narrow"))
    )
    rows = functions.reshape(FUN_DEV, TILES, LANES).transpose(1, 0, 2).reshape(TILES * FUN_DEV, LANES)
    filtered = filter_twice(rows, potential, cheb_coef)
    filtered, other = lax.optimization_barrier((filtered, other))
    mixer = dense_mixer(lax.axis_index("narrow"), kernel_halves, other, block_cols)
    outgoing = filtered.reshape(devices, own // LANES, FUN_DEV, LANES).transpose(0, 2, 1, 3)
    outgoing = outgoing.reshape(devices, FUN_DEV, own)
    points = lax.all_to_all(outgoing, ("narrow", "wide"), split_axis=0, concat_axis=0, tiled=True)
    mixed = mix_twice(mixer, points.reshape(FUNCS, own))
    result = lax.all_to_all(
        mixed.reshape(devices, FUN_DEV, own), ("narrow", "wide"), split_axis=0, concat_axis=0, tiled=True
    )
    return result.transpose(1, 0, 2).reshape(FUN_DEV, GRID)


def solution(mesh):
    return jax.shard_map(
        local,
        mesh=mesh,
        in_specs=(P(("wide", "narrow"), None), P(), P(), P(), P("narrow", None, None, None)),
        out_specs=P(("wide", "narrow"), None),
        check_vma=False,
    )
```

```python
import jax
import jax.numpy as jnp
from jax import lax
from jax.experimental import pallas as pl
from jax.experimental.pallas import tpu as pltpu
from jax.sharding import PartitionSpec as P

FUN_DEV = 4
BOX_X = 64
BOX_Y = 32
BOX_Z = 32
BLOCK = 64
DEGREE = 8
UPDATES = 2
GRID = 65536
FUNCS = 1024
LANES = 128
SUBLANES = 8
X_FAR = 2
X_IN = 8
PARTS = 16
Y_OUT = BOX_Y * BOX_Z // LANES
TILES = GRID // LANES


def swap_chunks(group, lane):
    low = lane < 64
    even = (lane // 32) % 2 == 0
    upper, lower = [], []
    for first, second in ((group[0], group[2]), (group[1], group[3])):
        upper.append(jnp.where(low, first, pltpu.roll(second, 64, 1)))
        lower.append(jnp.where(low, pltpu.roll(first, 64, 1), second))
    out = []
    for first, second in (upper, lower):
        out.append(jnp.where(even, first, pltpu.roll(second, 32, 1)))
        out.append(jnp.where(even, pltpu.roll(first, 96, 1), second))
    return out


def point_order(size):
    first = lax.broadcasted_iota(jnp.int32, (size, size), 0)
    second = lax.broadcasted_iota(jnp.int32, (size, size), 1)
    column = first // 32 * 32 + first % 8 * 4 + first // 8 % 4
    return (second == column).astype(jnp.float32).astype(jnp.bfloat16)


def filter_kernel(
    coef_hbm,
    potential_hbm,
    in_hbm,
    out_ref,
    coef_ref,
    potential_ref,
    in_ref,
    plane_ref,
    turned_ref,
    shift_ref,
    field_ref,
    even_ref,
    odd_ref,
    semaphores,
):
    arrivals = [
        pltpu.make_async_copy(source, target, semaphores.at[index])
        for index, (source, target) in enumerate(
            ((potential_hbm, potential_ref), (in_hbm, in_ref), (coef_hbm, coef_ref))
        )
    ]
    for arrival in arrivals:
        arrival.start()
    lane = lax.broadcasted_iota(jnp.int32, (SUBLANES, LANES), 1)
    row = lax.broadcasted_iota(jnp.int32, (SUBLANES, LANES), 0)
    y_out = (lane // FUN_DEV) % Y_OUT
    order_z = point_order(LANES)
    first = lax.broadcasted_iota(jnp.int32, (LANES, LANES), 0)
    second = lax.broadcasted_iota(jnp.int32, (LANES, LANES), 1)
    unit = (first == second).astype(jnp.float32).astype(jnp.bfloat16)
    x_rows = Y_OUT * FUN_DEV

    arrivals[0].wait()
    for yo in range(Y_OUT):
        for xo in range(BOX_X // SUBLANES):
            shifted = 0.5 * (potential_ref[xo * SUBLANES:(xo + 1) * SUBLANES, yo * LANES:(yo + 1) * LANES] - 1.0)
            for fun in range(FUN_DEV):
                start = xo * SUBLANES * x_rows + yo * FUN_DEV + fun
                plane_ref[pl.ds(start, SUBLANES, stride=x_rows), :] = shifted

    def rows_of(far, xi, out):
        return pl.ds((far * 32 + out * X_IN + xi) * x_rows, x_rows)

    arrivals[1].wait()
    for xi in range(X_IN):
        blocks = [(far, out) for far in range(X_FAR) for out in range(4)]
        fields = jnp.concatenate([in_ref[rows_of(far, xi, out), :] for far, out in blocks], 0)
        fields = lax.dot_general(order_z, fields, (((1,), (1,)), ((), ())), preferred_element_type=jnp.float32)
        for far in range(X_FAR):
            field_ref[far, xi] = fields[:, far * LANES:(far + 1) * LANES].reshape(PARTS, SUBLANES, LANES)
            shifts = jnp.concatenate([plane_ref[rows_of(far, xi, out), :] for out in range(4)], 0)
            turned_ref[far] = shifts.T
            for part in range(PARTS):
                shift_ref[far, xi, part] = turned_ref[far, pl.ds(part // 4 * 32 + part % 4, SUBLANES, stride=4), :]

    def plane_step(before, at, after, target, coefficient, scale, last, start, far, xi):
        for part in range(PARTS):
            yi, zi = part // 4, part % 4
            total = before[part] + after[part]
            if zi < 3:
                total = total + at[part + 1]
            else:
                total = total + jnp.where(row < SUBLANES - 1, pltpu.roll(at[yi * 4], SUBLANES - 1, 0), 0.0)
            if zi > 0:
                total = total + at[part - 1]
            else:
                total = total + jnp.where(row > 0, pltpu.roll(at[yi * 4 + 3], 1, 0), 0.0)
            if yi < 3:
                total = total + at[part + 4]
            else:
                total = total + jnp.where(y_out < Y_OUT - 1, pltpu.roll(at[zi], LANES - FUN_DEV, 1), 0.0)
            if yi > 0:
                total = total + at[part - 4]
            else:
                total = total + jnp.where(y_out > 0, pltpu.roll(at[12 + zi], FUN_DEV, 1), 0.0)
            applied = shift_ref[far, xi, part] * at[part] - 0.25 * total
            if scale is not None:
                applied = scale * applied
            value = coefficient * field_ref[far, xi, part] + applied
            if not start:
                value = value - target[far, xi, part]
            if last:
                field_ref[far, xi, part] = value
            else:
                target[far, xi, part] = value

    def stencil_step(source, target, coefficient, scale=None, last=False, start=False):
        def plane(far, xi):
            return [source[far, xi, part] for part in range(PARTS)]

        def below(far):
            own = [pltpu.roll(v, 32, 1) for v in plane(far, X_IN - 1)]
            if far == 0:
                return [jnp.where(lane < 32, 0.0, v) for v in own]
            return [jnp.where(lane < 32, pltpu.roll(v, 32, 1), w) for v, w in zip(plane(0, X_IN - 1), own)]

        def above(far):
            own = [pltpu.roll(v, 96, 1) for v in plane(far, 0)]
            if far == 1:
                return [jnp.where(lane >= 96, 0.0, v) for v in own]
            return [jnp.where(lane >= 96, pltpu.roll(v, 96, 1), w) for v, w in zip(plane(1, 0), own)]

        for far in range(X_FAR):
            before, at = below(far), plane(far, 0)
            for xi in range(X_IN):
                after = plane(far, xi + 1) if xi < X_IN - 1 else above(far)
                plane_step(before, at, after, target, coefficient, scale, last, start, far, xi)
                before, at = at, after

    def one_update(update, carry):
        stencil_step(field_ref, odd_ref, coef_ref[DEGREE - 1], scale=coef_ref[DEGREE], start=True)
        stencil_step(odd_ref, even_ref, coef_ref[DEGREE - 2] - coef_ref[DEGREE], start=True)

        def two_orders(pair, carry):
            order = DEGREE - 3 - 2 * pair
            stencil_step(even_ref, odd_ref, coef_ref[order])
            stencil_step(odd_ref, even_ref, coef_ref[order - 1])
            return carry

        lax.fori_loop(0, DEGREE // 2 - 2, two_orders, 0)
        stencil_step(even_ref, odd_ref, coef_ref[1])
        stencil_step(odd_ref, even_ref, coef_ref[0], scale=0.5, last=True)
        return carry

    arrivals[2].wait()
    lax.fori_loop(0, UPDATES, one_update, 0)

    for xi in range(X_IN):
        fields = field_ref[:, xi].reshape(X_FAR * LANES, LANES).astype(jnp.bfloat16)
        fields = lax.dot_general(unit, fields, (((1,), (1,)), ((), ())), preferred_element_type=jnp.float32)
        fields = fields.astype(jnp.bfloat16)
        for far in range(X_FAR):
            for out in range(4):
                rows = fields[out * x_rows:(out + 1) * x_rows, far * LANES:(far + 1) * LANES]
                out_ref[rows_of(far, xi, out), :] = rows


def filter_twice(rows, potential, coefficient):
    vectors = pltpu.VMEM((X_FAR, X_IN, PARTS, SUBLANES, LANES), jnp.float32)
    return pl.pallas_call(
        filter_kernel,
        name="filter_twice",
        out_shape=jax.ShapeDtypeStruct(rows.shape, jnp.bfloat16),
        in_specs=[pl.BlockSpec(memory_space=pltpu.HBM)] * 3,
        out_specs=pl.BlockSpec(memory_space=pltpu.VMEM),
        scratch_shapes=[
            pltpu.SMEM(coefficient.shape, jnp.float32),
            pltpu.VMEM(potential.shape, jnp.float32),
            pltpu.VMEM(rows.shape, jnp.bfloat16),
            pltpu.VMEM(rows.shape, jnp.float32),
            pltpu.VMEM((X_FAR, LANES, LANES), jnp.float32),
            vectors,
            vectors,
            vectors,
            vectors,
            pltpu.SemaphoreType.DMA((3,)),
        ],
        compiler_params=pltpu.CompilerParams(vmem_limit_bytes=60 * 2**20),
        cost_estimate=pl.CostEstimate(flops=60_000_000, bytes_accessed=40_000_000, transcendentals=0),
    )(coefficient, potential, rows)


def mix_kernel(mixer_ref, points_ref, out_ref, middle_ref):
    size = points_ref.shape[1]
    points = jnp.dot(points_ref[...], point_order(size), preferred_element_type=jnp.float32).astype(jnp.bfloat16)
    for start in range(0, FUNCS, size):
        part = jnp.dot(mixer_ref[start:start + size, :], points, preferred_element_type=jnp.float32)
        middle_ref[start:start + size, :] = part.astype(jnp.bfloat16)
    points = middle_ref[...]
    for start in range(0, FUNCS, size):
        part = jnp.dot(mixer_ref[start:start + size, :], points, preferred_element_type=jnp.float32)
        out_ref[start:start + size, :] = part.astype(jnp.bfloat16)


def mix_twice(mixer, points):
    return pl.pallas_call(
        mix_kernel,
        name="mix_twice",
        out_shape=jax.ShapeDtypeStruct(points.shape, jnp.bfloat16),
        in_specs=[pl.BlockSpec(memory_space=pltpu.VMEM)] * 2,
        out_specs=pl.BlockSpec(memory_space=pltpu.VMEM),
        scratch_shapes=[pltpu.VMEM(points.shape, jnp.bfloat16)],
        compiler_params=pltpu.CompilerParams(vmem_limit_bytes=24 * 2**20),
        cost_estimate=pl.CostEstimate(flops=1_100_000_000, bytes_accessed=4_000_000, transcendentals=0),
    )(mixer, points)


def spread_kernel(half_ref, place_ref, swapped_ref, own_ref, near_ref, far_ref, out_ref, wide_ref):
    lane = lax.broadcasted_iota(jnp.int32, (SUBLANES, LANES), 1)
    row_blocks = FUNCS // BLOCK
    column_tiles = FUNCS // 2 // LANES
    sides = (
        (place_ref, (own_ref,), half_ref[0]),
        (swapped_ref, (near_ref, far_ref), 1 - half_ref[0]),
    )

    def one_pair(pair, carry):
        columns = pl.ds(pl.multiple_of(pair * 2 * LANES, 2 * LANES), 2 * LANES)
        spreads = []
        for where_ref, source_refs, _ in sides:
            entries = jnp.concatenate([source_ref[:, columns] for source_ref in source_refs], 0)
            spreads.append(jnp.dot(where_ref[...], entries, preferred_element_type=jnp.float32))
        for spread, (_, _, half) in zip(spreads, sides):
            for side in range(2):
                for tile in range(column_tiles):
                    for rows in range(row_blocks // SUBLANES):
                        group = [
                            spread[
                                (tile * 4 + step) * row_blocks + rows * SUBLANES:
                                (tile * 4 + step) * row_blocks + (rows + 1) * SUBLANES,
                                side * LANES:(side + 1) * LANES,
                            ]
                            for step in range(4)
                        ]
                        for fun, value in enumerate(swap_chunks(group, lane)):
                            start = (half * column_tiles + tile) * FUNCS
                            start = start + side * (FUNCS // 2) + rows * SUBLANES * (BLOCK // 2) + pair * FUN_DEV + fun
                            wide_ref[pl.ds(start, SUBLANES, stride=BLOCK // 2), :] = value
        return carry

    lax.fori_loop(0, BLOCK * BLOCK // 2 // (2 * LANES), one_pair, 0)
    for tile in range(FUNCS // LANES):
        out_ref[:, tile * LANES:(tile + 1) * LANES] = wide_ref[tile * FUNCS:(tile + 1) * FUNCS, :].astype(jnp.bfloat16)


def dense_mixer(half, core, own, near, far, block_cols):
    row_blocks, slots = block_cols.shape
    entry = jnp.arange(slots * row_blocks)
    place = jnp.arange(row_blocks * row_blocks)
    column = block_cols.T.reshape(-1)
    cut = column.shape[0] // 2
    swapped = jnp.where(core == 0, column, jnp.concatenate([column[cut:], column[:cut]]))

    def chosen(column):
        return (
            (column[None, :] == place[:, None] // row_blocks)
            & (entry[None, :] % row_blocks == place[:, None] % row_blocks)
        ).astype(jnp.bfloat16)

    def flat(blocks):
        return blocks[0].transpose(1, 0, 2).reshape(-1, BLOCK * BLOCK // 2)

    return pl.pallas_call(
        spread_kernel,
        name="spread_blocks",
        out_shape=jax.ShapeDtypeStruct((FUNCS, FUNCS), jnp.bfloat16),
        in_specs=[pl.BlockSpec(memory_space=pltpu.SMEM)] + [pl.BlockSpec(memory_space=pltpu.VMEM)] * 5,
        out_specs=pl.BlockSpec(memory_space=pltpu.VMEM),
        scratch_shapes=[pltpu.VMEM((FUNCS * FUNCS // LANES, LANES), jnp.float32)],
        compiler_params=pltpu.CompilerParams(vmem_limit_bytes=60 * 2**20),
        cost_estimate=pl.CostEstimate(flops=400_000_000, bytes_accessed=15_000_000, transcendentals=0),
    )(half.reshape(1), chosen(column), chosen(swapped), flat(own), flat(near), flat(far))


def other_half_pairs(wide, narrow):
    pairs = []
    for target in range(wide * narrow):
        rest, low = divmod(target, 2)
        rest, core = divmod(rest, 2)
        rest, z = divmod(rest, 8)
        x, high = divmod(rest, 2)
        y = (high * 2 + low + (1 if core == 0 else 3)) % 4
        pairs.append(((((x * 2 + y // 2) * 8 + z) * 2 + core) * 2 + y % 2, target))
    return pairs


def local(functions, potential, cheb_coef, block_cols, kernel_halves):
    devices = lax.axis_size("wide") * lax.axis_size("narrow")
    own = GRID // devices
    wide, narrow = lax.axis_size("wide"), lax.axis_size("narrow")
    core = lax.axis_index("wide") % 2
    slots = kernel_halves.shape[2] // 2
    part = lax.dynamic_slice_in_dim(kernel_halves, core * slots, slots, 2)
    near = lax.ppermute(part, ("wide", "narrow"), other_half_pairs(wide, narrow))
    rows = functions.reshape(FUN_DEV, TILES, LANES).transpose(1, 0, 2).reshape(TILES * FUN_DEV, LANES)
    filtered = filter_twice(rows, potential, cheb_coef)
    filtered, near = lax.optimization_barrier((filtered, near))
    far = lax.ppermute(near, "wide", [(index, index ^ 1) for index in range(wide)])
    mixer = dense_mixer(lax.axis_index("narrow"), core, kernel_halves, near, far, block_cols)
    outgoing = filtered.reshape(devices, own // LANES, FUN_DEV, LANES).transpose(0, 2, 1, 3)
    outgoing = outgoing.reshape(devices, FUN_DEV, own)
    points = lax.all_to_all(outgoing, ("narrow", "wide"), split_axis=0, concat_axis=0, tiled=True)
    mixed = mix_twice(mixer, points.reshape(FUNCS, own))
    result = lax.all_to_all(
        mixed.reshape(devices, FUN_DEV, own), ("narrow", "wide"), split_axis=0, concat_axis=0, tiled=True
    )
    return result.transpose(1, 0, 2).reshape(FUN_DEV, GRID)


def solution(mesh):
    return jax.shard_map(
        local,
        mesh=mesh,
        in_specs=(P(("wide", "narrow"), None), P(), P(), P(), P("narrow", None, None, None)),
        out_specs=P(("wide", "narrow"), None),
        check_vma=False,
    )
```

```python
import jax
import jax.numpy as jnp
from jax import lax
from jax.experimental import pallas as pl
from jax.experimental.pallas import tpu as pltpu
from jax.sharding import PartitionSpec as P

FUN_DEV = 4
BOX_X = 64
BOX_Y = 32
BOX_Z = 32
BLOCK = 64
DEGREE = 8
UPDATES = 2
GRID = 65536
FUNCS = 1024
LANES = 128
SUBLANES = 8
X_FAR = 2
X_IN = 8
PARTS = 16
Y_OUT = BOX_Y * BOX_Z // LANES
TILES = GRID // LANES


def swap_chunks(group, lane):
    low = lane < 64
    even = (lane // 32) % 2 == 0
    upper, lower = [], []
    for first, second in ((group[0], group[2]), (group[1], group[3])):
        upper.append(jnp.where(low, first, pltpu.roll(second, 64, 1)))
        lower.append(jnp.where(low, pltpu.roll(first, 64, 1), second))
    out = []
    for first, second in (upper, lower):
        out.append(jnp.where(even, first, pltpu.roll(second, 32, 1)))
        out.append(jnp.where(even, pltpu.roll(first, 96, 1), second))
    return out


def point_order(size):
    first = lax.broadcasted_iota(jnp.int32, (size, size), 0)
    second = lax.broadcasted_iota(jnp.int32, (size, size), 1)
    column = first // 32 * 32 + first % 8 * 4 + first // 8 % 4
    return (second == column).astype(jnp.float32).astype(jnp.bfloat16)


def filter_kernel(
    coef_hbm,
    potential_hbm,
    in_hbm,
    out_ref,
    coef_ref,
    potential_ref,
    in_ref,
    plane_ref,
    turned_ref,
    shift_ref,
    field_ref,
    even_ref,
    odd_ref,
    semaphores,
):
    arrivals = [
        pltpu.make_async_copy(source, target, semaphores.at[index])
        for index, (source, target) in enumerate(
            ((potential_hbm, potential_ref), (in_hbm, in_ref), (coef_hbm, coef_ref))
        )
    ]
    for arrival in arrivals:
        arrival.start()
    lane = lax.broadcasted_iota(jnp.int32, (SUBLANES, LANES), 1)
    row = lax.broadcasted_iota(jnp.int32, (SUBLANES, LANES), 0)
    y_out = (lane // FUN_DEV) % Y_OUT
    order_z = point_order(LANES)
    first = lax.broadcasted_iota(jnp.int32, (LANES, LANES), 0)
    second = lax.broadcasted_iota(jnp.int32, (LANES, LANES), 1)
    unit = (first == second).astype(jnp.float32).astype(jnp.bfloat16)
    x_rows = Y_OUT * FUN_DEV

    arrivals[0].wait()
    for yo in range(Y_OUT):
        for xo in range(BOX_X // SUBLANES):
            shifted = 0.5 * (potential_ref[xo * SUBLANES:(xo + 1) * SUBLANES, yo * LANES:(yo + 1) * LANES] - 1.0)
            for fun in range(FUN_DEV):
                start = xo * SUBLANES * x_rows + yo * FUN_DEV + fun
                plane_ref[pl.ds(start, SUBLANES, stride=x_rows), :] = shifted

    def rows_of(far, xi, out):
        return pl.ds((far * 32 + out * X_IN + xi) * x_rows, x_rows)

    arrivals[1].wait()
    for xi in range(X_IN):
        blocks = [(far, out) for far in range(X_FAR) for out in range(4)]
        fields = jnp.concatenate([in_ref[rows_of(far, xi, out), :] for far, out in blocks], 0)
        fields = lax.dot_general(order_z, fields, (((1,), (1,)), ((), ())), preferred_element_type=jnp.float32)
        for far in range(X_FAR):
            field_ref[far, xi] = fields[:, far * LANES:(far + 1) * LANES].reshape(PARTS, SUBLANES, LANES)
            shifts = jnp.concatenate([plane_ref[rows_of(far, xi, out), :] for out in range(4)], 0)
            turned_ref[far] = shifts.T
            for part in range(PARTS):
                shift_ref[far, xi, part] = turned_ref[far, pl.ds(part // 4 * 32 + part % 4, SUBLANES, stride=4), :]

    def plane_step(before, at, after, target, coefficient, scale, last, start, far, xi):
        near = {(part // 4, part % 4): at[part] for part in range(PARTS)}
        for index in range(4):
            near[index, 4] = jnp.where(row < SUBLANES - 1, pltpu.roll(near[index, 0], SUBLANES - 1, 0), 0.0)
            near[index, -1] = jnp.where(row > 0, pltpu.roll(near[index, 3], 1, 0), 0.0)
            near[4, index] = jnp.where(y_out < Y_OUT - 1, pltpu.roll(near[0, index], LANES - FUN_DEV, 1), 0.0)
            near[-1, index] = jnp.where(y_out > 0, pltpu.roll(near[3, index], FUN_DEV, 1), 0.0)
        ahead = {}
        for yi in range(-1, 4):
            for zi in range(-1, 4):
                if (yi, zi) not in ((-1, 3), (3, -1)):
                    ahead[yi, zi] = near[yi, zi + 1] + near[yi + 1, zi]
        for part in range(PARTS):
            yi, zi = part // 4, part % 4
            total = before[part] + after[part] + (ahead[yi, zi] + ahead[yi - 1, zi - 1])
            applied = shift_ref[far, xi, part] * at[part] - 0.25 * total
            if scale is not None:
                applied = scale * applied
            value = coefficient * field_ref[far, xi, part] + applied
            if not start:
                value = value - target[far, xi, part]
            if last:
                field_ref[far, xi, part] = value
            else:
                target[far, xi, part] = value

    def stencil_step(source, target, coefficient, scale=None, last=False, start=False):
        def plane(far, xi):
            return [source[far, xi, part] for part in range(PARTS)]

        def below(far):
            own = [pltpu.roll(v, 32, 1) for v in plane(far, X_IN - 1)]
            if far == 0:
                return [jnp.where(lane < 32, 0.0, v) for v in own]
            return [jnp.where(lane < 32, pltpu.roll(v, 32, 1), w) for v, w in zip(plane(0, X_IN - 1), own)]

        def above(far):
            own = [pltpu.roll(v, 96, 1) for v in plane(far, 0)]
            if far == 1:
                return [jnp.where(lane >= 96, 0.0, v) for v in own]
            return [jnp.where(lane >= 96, pltpu.roll(v, 96, 1), w) for v, w in zip(plane(1, 0), own)]

        for far in range(X_FAR):
            before, at = below(far), plane(far, 0)
            for xi in range(X_IN):
                after = plane(far, xi + 1) if xi < X_IN - 1 else above(far)
                plane_step(before, at, after, target, coefficient, scale, last, start, far, xi)
                before, at = at, after

    def one_update(update, carry):
        stencil_step(field_ref, odd_ref, coef_ref[DEGREE - 1], scale=coef_ref[DEGREE], start=True)
        stencil_step(odd_ref, even_ref, coef_ref[DEGREE - 2] - coef_ref[DEGREE], start=True)

        def two_orders(pair, carry):
            order = DEGREE - 3 - 2 * pair
            stencil_step(even_ref, odd_ref, coef_ref[order])
            stencil_step(odd_ref, even_ref, coef_ref[order - 1])
            return carry

        lax.fori_loop(0, DEGREE // 2 - 2, two_orders, 0)
        stencil_step(even_ref, odd_ref, coef_ref[1])
        stencil_step(odd_ref, even_ref, coef_ref[0], scale=0.5, last=True)
        return carry

    arrivals[2].wait()
    lax.fori_loop(0, UPDATES, one_update, 0)

    for xi in range(X_IN):
        fields = field_ref[:, xi].reshape(X_FAR * LANES, LANES).astype(jnp.bfloat16)
        fields = lax.dot_general(unit, fields, (((1,), (1,)), ((), ())), preferred_element_type=jnp.float32)
        fields = fields.astype(jnp.bfloat16)
        for far in range(X_FAR):
            for out in range(4):
                rows = fields[out * x_rows:(out + 1) * x_rows, far * LANES:(far + 1) * LANES]
                out_ref[rows_of(far, xi, out), :] = rows


def filter_twice(rows, potential, coefficient):
    vectors = pltpu.VMEM((X_FAR, X_IN, PARTS, SUBLANES, LANES), jnp.float32)
    return pl.pallas_call(
        filter_kernel,
        name="filter_twice",
        out_shape=jax.ShapeDtypeStruct(rows.shape, jnp.bfloat16),
        in_specs=[pl.BlockSpec(memory_space=pltpu.HBM)] * 3,
        out_specs=pl.BlockSpec(memory_space=pltpu.VMEM),
        scratch_shapes=[
            pltpu.SMEM(coefficient.shape, jnp.float32),
            pltpu.VMEM(potential.shape, jnp.float32),
            pltpu.VMEM(rows.shape, jnp.bfloat16),
            pltpu.VMEM(rows.shape, jnp.float32),
            pltpu.VMEM((X_FAR, LANES, LANES), jnp.float32),
            vectors,
            vectors,
            vectors,
            vectors,
            pltpu.SemaphoreType.DMA((3,)),
        ],
        compiler_params=pltpu.CompilerParams(vmem_limit_bytes=60 * 2**20),
        cost_estimate=pl.CostEstimate(flops=60_000_000, bytes_accessed=40_000_000, transcendentals=0),
    )(coefficient, potential, rows)


def mix_kernel(mixer_ref, points_ref, out_ref, middle_ref):
    size = points_ref.shape[1]
    points = jnp.dot(points_ref[...], point_order(size), preferred_element_type=jnp.float32).astype(jnp.bfloat16)
    for start in range(0, FUNCS, size):
        part = jnp.dot(mixer_ref[start:start + size, :], points, preferred_element_type=jnp.float32)
        middle_ref[start:start + size, :] = part.astype(jnp.bfloat16)
    points = middle_ref[...]
    for start in range(0, FUNCS, size):
        part = jnp.dot(mixer_ref[start:start + size, :], points, preferred_element_type=jnp.float32)
        out_ref[start:start + size, :] = part.astype(jnp.bfloat16)


def mix_twice(mixer, points):
    return pl.pallas_call(
        mix_kernel,
        name="mix_twice",
        out_shape=jax.ShapeDtypeStruct(points.shape, jnp.bfloat16),
        in_specs=[pl.BlockSpec(memory_space=pltpu.VMEM)] * 2,
        out_specs=pl.BlockSpec(memory_space=pltpu.VMEM),
        scratch_shapes=[pltpu.VMEM(points.shape, jnp.bfloat16)],
        compiler_params=pltpu.CompilerParams(vmem_limit_bytes=24 * 2**20),
        cost_estimate=pl.CostEstimate(flops=1_100_000_000, bytes_accessed=4_000_000, transcendentals=0),
    )(mixer, points)


def spread_kernel(half_ref, place_ref, own_ref, other_ref, out_ref, wide_ref):
    lane = lax.broadcasted_iota(jnp.int32, (SUBLANES, LANES), 1)
    row_blocks = FUNCS // BLOCK
    column_tiles = FUNCS // 2 // LANES
    sides = ((own_ref, half_ref[0]), (other_ref, 1 - half_ref[0]))

    def one_pair(pair, carry):
        columns = pl.ds(pl.multiple_of(pair * 2 * LANES, 2 * LANES), 2 * LANES)
        spreads = []
        for source_ref, _ in sides:
            spreads.append(jnp.dot(place_ref[...], source_ref[:, columns], preferred_element_type=jnp.float32))
        for spread, (_, half) in zip(spreads, sides):
            for side in range(2):
                for tile in range(column_tiles):
                    for rows in range(row_blocks // SUBLANES):
                        group = [
                            spread[
                                (tile * 4 + step) * row_blocks + rows * SUBLANES:
                                (tile * 4 + step) * row_blocks + (rows + 1) * SUBLANES,
                                side * LANES:(side + 1) * LANES,
                            ]
                            for step in range(4)
                        ]
                        for fun, value in enumerate(swap_chunks(group, lane)):
                            start = (half * column_tiles + tile) * FUNCS
                            start = start + side * (FUNCS // 2) + rows * SUBLANES * (BLOCK // 2) + pair * FUN_DEV + fun
                            wide_ref[pl.ds(start, SUBLANES, stride=BLOCK // 2), :] = value
        return carry

    lax.fori_loop(0, BLOCK * BLOCK // 2 // (2 * LANES), one_pair, 0)
    for tile in range(FUNCS // LANES):
        out_ref[:, tile * LANES:(tile + 1) * LANES] = wide_ref[tile * FUNCS:(tile + 1) * FUNCS, :].astype(jnp.bfloat16)


def dense_mixer(half, own, other, block_cols):
    row_blocks, slots = block_cols.shape
    entry = jnp.arange(slots * row_blocks)
    place = jnp.arange(row_blocks * row_blocks)
    column = block_cols.T.reshape(-1)
    chosen = (column[None, :] == place[:, None] // row_blocks) & (
        entry[None, :] % row_blocks == place[:, None] % row_blocks
    )

    def flat(blocks):
        return blocks[0].transpose(1, 0, 2).reshape(slots * row_blocks, BLOCK * BLOCK // 2)

    return pl.pallas_call(
        spread_kernel,
        name="spread_blocks",
        out_shape=jax.ShapeDtypeStruct((FUNCS, FUNCS), jnp.bfloat16),
        in_specs=[pl.BlockSpec(memory_space=pltpu.SMEM)] + [pl.BlockSpec(memory_space=pltpu.VMEM)] * 3,
        out_specs=pl.BlockSpec(memory_space=pltpu.VMEM),
        scratch_shapes=[pltpu.VMEM((FUNCS * FUNCS // LANES, LANES), jnp.float32)],
        compiler_params=pltpu.CompilerParams(vmem_limit_bytes=16 * 2**20),
        cost_estimate=pl.CostEstimate(flops=400_000_000, bytes_accessed=15_000_000, transcendentals=0),
    )(half.reshape(1), chosen.astype(jnp.bfloat16), flat(own), flat(other))


def other_half_pairs(wide, narrow):
    pairs = []
    for target in range(wide * narrow):
        rest, low = divmod(target, 2)
        rest, core = divmod(rest, 2)
        rest, z = divmod(rest, 8)
        x, high = divmod(rest, 2)
        y = (high * 2 + low + (1 if core == 0 else 3)) % 4
        pairs.append(((((x * 2 + y // 2) * 8 + z) * 2 + core) * 2 + y % 2, target))
    return pairs


def local(functions, potential, cheb_coef, block_cols, kernel_halves):
    devices = lax.axis_size("wide") * lax.axis_size("narrow")
    own = GRID // devices
    other = lax.ppermute(
        kernel_halves, ("wide", "narrow"), other_half_pairs(lax.axis_size("wide"), lax.axis_size("narrow"))
    )
    rows = functions.reshape(FUN_DEV, TILES, LANES).transpose(1, 0, 2).reshape(TILES * FUN_DEV, LANES)
    filtered = filter_twice(rows, potential, cheb_coef)
    filtered, other = lax.optimization_barrier((filtered, other))
    mixer = dense_mixer(lax.axis_index("narrow"), kernel_halves, other, block_cols)
    outgoing = filtered.reshape(devices, own // LANES, FUN_DEV, LANES).transpose(0, 2, 1, 3)
    outgoing = outgoing.reshape(devices, FUN_DEV, own)
    points = lax.all_to_all(outgoing, ("narrow", "wide"), split_axis=0, concat_axis=0, tiled=True)
    mixed = mix_twice(mixer, points.reshape(FUNCS, own))
    result = lax.all_to_all(
        mixed.reshape(devices, FUN_DEV, own), ("narrow", "wide"), split_axis=0, concat_axis=0, tiled=True
    )
    return result.transpose(1, 0, 2).reshape(FUN_DEV, GRID)


def solution(mesh):
    return jax.shard_map(
        local,
        mesh=mesh,
        in_specs=(P(("wide", "narrow"), None), P(), P(), P(), P("narrow", None, None, None)),
        out_specs=P(("wide", "narrow"), None),
        check_vma=False,
    )
```

```python
import jax
import jax.numpy as jnp
from jax import lax
from jax.experimental import pallas as pl
from jax.experimental.pallas import tpu as pltpu
from jax.sharding import PartitionSpec as P

FUN_DEV = 4
BOX_X = 64
BOX_Y = 32
BOX_Z = 32
BLOCK = 64
DEGREE = 8
UPDATES = 2
GRID = 65536
FUNCS = 1024
LANES = 128
SUBLANES = 8
X_FAR = 2
X_IN = 8
PARTS = 16
Y_OUT = BOX_Y * BOX_Z // LANES
TILES = GRID // LANES


def swap_chunks(group, lane):
    low = lane < 64
    even = (lane // 32) % 2 == 0
    upper, lower = [], []
    for first, second in ((group[0], group[2]), (group[1], group[3])):
        upper.append(jnp.where(low, first, pltpu.roll(second, 64, 1)))
        lower.append(jnp.where(low, pltpu.roll(first, 64, 1), second))
    out = []
    for first, second in (upper, lower):
        out.append(jnp.where(even, first, pltpu.roll(second, 32, 1)))
        out.append(jnp.where(even, pltpu.roll(first, 96, 1), second))
    return out


def point_order(size):
    first = lax.broadcasted_iota(jnp.int32, (size, size), 0)
    second = lax.broadcasted_iota(jnp.int32, (size, size), 1)
    column = first // 32 * 32 + first % 8 * 4 + first // 8 % 4
    return (second == column).astype(jnp.float32).astype(jnp.bfloat16)


def filter_kernel(
    coef_hbm,
    potential_hbm,
    in_hbm,
    out_ref,
    coef_ref,
    potential_ref,
    in_ref,
    plane_ref,
    turned_ref,
    shift_ref,
    field_ref,
    even_ref,
    odd_ref,
    semaphores,
):
    arrivals = [
        pltpu.make_async_copy(source, target, semaphores.at[index])
        for index, (source, target) in enumerate(
            ((potential_hbm, potential_ref), (in_hbm, in_ref), (coef_hbm, coef_ref))
        )
    ]
    for arrival in arrivals:
        arrival.start()
    lane = lax.broadcasted_iota(jnp.int32, (SUBLANES, LANES), 1)
    row = lax.broadcasted_iota(jnp.int32, (SUBLANES, LANES), 0)
    y_out = (lane // FUN_DEV) % Y_OUT
    order_z = point_order(LANES)
    first = lax.broadcasted_iota(jnp.int32, (LANES, LANES), 0)
    second = lax.broadcasted_iota(jnp.int32, (LANES, LANES), 1)
    unit = (first == second).astype(jnp.float32).astype(jnp.bfloat16)
    x_rows = Y_OUT * FUN_DEV

    arrivals[0].wait()
    for yo in range(Y_OUT):
        for xo in range(BOX_X // SUBLANES):
            shifted = 0.5 * (potential_ref[xo * SUBLANES:(xo + 1) * SUBLANES, yo * LANES:(yo + 1) * LANES] - 1.0)
            for fun in range(FUN_DEV):
                start = xo * SUBLANES * x_rows + yo * FUN_DEV + fun
                plane_ref[pl.ds(start, SUBLANES, stride=x_rows), :] = shifted

    def rows_of(far, xi, out):
        return pl.ds((far * 32 + out * X_IN + xi) * x_rows, x_rows)

    arrivals[1].wait()
    for xi in range(X_IN):
        blocks = [(far, out) for far in range(X_FAR) for out in range(4)]
        fields = jnp.concatenate([in_ref[rows_of(far, xi, out), :] for far, out in blocks], 0)
        fields = lax.dot_general(order_z, fields, (((1,), (1,)), ((), ())), preferred_element_type=jnp.float32)
        for far in range(X_FAR):
            field_ref[far, xi] = fields[:, far * LANES:(far + 1) * LANES].reshape(PARTS, SUBLANES, LANES)
            shifts = jnp.concatenate([plane_ref[rows_of(far, xi, out), :] for out in range(4)], 0)
            turned_ref[far] = shifts.T
            for part in range(PARTS):
                shift_ref[far, xi, part] = turned_ref[far, pl.ds(part // 4 * 32 + part % 4, SUBLANES, stride=4), :]

    def plane_step(before, at, after, target, coefficient, scale, last, start, far, xi):
        near = {(part // 4, part % 4): at[part] for part in range(PARTS)}
        for index in range(4):
            near[index, 4] = jnp.where(row < SUBLANES - 1, pltpu.roll(near[index, 0], SUBLANES - 1, 0), 0.0)
            near[index, -1] = jnp.where(row > 0, pltpu.roll(near[index, 3], 1, 0), 0.0)
            near[4, index] = jnp.where(y_out < Y_OUT - 1, pltpu.roll(near[0, index], LANES - FUN_DEV, 1), 0.0)
            near[-1, index] = jnp.where(y_out > 0, pltpu.roll(near[3, index], FUN_DEV, 1), 0.0)
        ahead = {}
        for yi in range(-1, 4):
            for zi in range(-1, 4):
                if (yi, zi) not in ((-1, 3), (3, -1)):
                    ahead[yi, zi] = near[yi, zi + 1] + near[yi + 1, zi]
        for part in range(PARTS):
            yi, zi = part // 4, part % 4
            total = before[part] + after[part] + (ahead[yi, zi] + ahead[yi - 1, zi - 1])
            applied = shift_ref[far, xi, part] * at[part] - 0.25 * total
            if scale is not None:
                applied = scale * applied
            value = coefficient * field_ref[far, xi, part] + applied
            if not start:
                value = value - target[far, xi, part]
            if last:
                field_ref[far, xi, part] = value
            else:
                target[far, xi, part] = value

    def stencil_step(source, target, coefficient, scale=None, last=False, start=False):
        def plane(far, xi):
            return [source[far, xi, part] for part in range(PARTS)]

        def below(far):
            own = [pltpu.roll(v, 32, 1) for v in plane(far, X_IN - 1)]
            if far == 0:
                return [jnp.where(lane < 32, 0.0, v) for v in own]
            return [jnp.where(lane < 32, pltpu.roll(v, 32, 1), w) for v, w in zip(plane(0, X_IN - 1), own)]

        def above(far):
            own = [pltpu.roll(v, 96, 1) for v in plane(far, 0)]
            if far == 1:
                return [jnp.where(lane >= 96, 0.0, v) for v in own]
            return [jnp.where(lane >= 96, pltpu.roll(v, 96, 1), w) for v, w in zip(plane(1, 0), own)]

        for far in range(X_FAR):
            before, at = below(far), plane(far, 0)
            for xi in range(X_IN):
                after = plane(far, xi + 1) if xi < X_IN - 1 else above(far)
                plane_step(before, at, after, target, coefficient, scale, last, start, far, xi)
                before, at = at, after

    def one_update(update, carry):
        stencil_step(field_ref, odd_ref, coef_ref[DEGREE - 1], scale=coef_ref[DEGREE], start=True)
        stencil_step(odd_ref, even_ref, coef_ref[DEGREE - 2] - coef_ref[DEGREE], start=True)

        def two_orders(pair, carry):
            order = DEGREE - 3 - 2 * pair
            stencil_step(even_ref, odd_ref, coef_ref[order])
            stencil_step(odd_ref, even_ref, coef_ref[order - 1])
            return carry

        lax.fori_loop(0, DEGREE // 2 - 2, two_orders, 0)
        stencil_step(even_ref, odd_ref, coef_ref[1])
        stencil_step(odd_ref, even_ref, coef_ref[0], scale=0.5, last=True)
        return carry

    arrivals[2].wait()
    lax.fori_loop(0, UPDATES, one_update, 0)

    for xi in range(X_IN):
        fields = field_ref[:, xi].reshape(X_FAR * LANES, LANES).astype(jnp.bfloat16)
        fields = lax.dot_general(unit, fields, (((1,), (1,)), ((), ())), preferred_element_type=jnp.float32)
        fields = fields.astype(jnp.bfloat16)
        for far in range(X_FAR):
            for out in range(4):
                rows = fields[out * x_rows:(out + 1) * x_rows, far * LANES:(far + 1) * LANES]
                out_ref[rows_of(far, xi, out), :] = rows


def filter_twice(rows, potential, coefficient):
    vectors = pltpu.VMEM((X_FAR, X_IN, PARTS, SUBLANES, LANES), jnp.float32)
    return pl.pallas_call(
        filter_kernel,
        name="filter_twice",
        out_shape=jax.ShapeDtypeStruct(rows.shape, jnp.bfloat16),
        in_specs=[pl.BlockSpec(memory_space=pltpu.HBM)] * 3,
        out_specs=pl.BlockSpec(memory_space=pltpu.VMEM),
        scratch_shapes=[
            pltpu.SMEM(coefficient.shape, jnp.float32),
            pltpu.VMEM(potential.shape, jnp.float32),
            pltpu.VMEM(rows.shape, jnp.bfloat16),
            pltpu.VMEM(rows.shape, jnp.float32),
            pltpu.VMEM((X_FAR, LANES, LANES), jnp.float32),
            vectors,
            vectors,
            vectors,
            vectors,
            pltpu.SemaphoreType.DMA((3,)),
        ],
        compiler_params=pltpu.CompilerParams(vmem_limit_bytes=60 * 2**20),
        cost_estimate=pl.CostEstimate(flops=60_000_000, bytes_accessed=40_000_000, transcendentals=0),
    )(coefficient, potential, rows)


def mix_kernel(half_ref, own_ref, other_ref, points_ref, out_ref, first_ref, middle_ref):
    size = points_ref.shape[1]
    points = jnp.dot(points_ref[...], point_order(size), preferred_element_type=jnp.float32)
    first_ref[...] = points.astype(jnp.bfloat16)
    count = FUNCS // 2
    for source_ref, target_ref in ((first_ref, middle_ref), (middle_ref, out_ref)):
        own = source_ref[pl.ds(pl.multiple_of(half_ref[0] * count, count), count), :]
        other = source_ref[pl.ds(pl.multiple_of((1 - half_ref[0]) * count, count), count), :]
        for start in range(0, FUNCS, size):
            rows = slice(start, start + size)
            part = jnp.dot(own_ref[rows, :], own, preferred_element_type=jnp.float32)
            part = part + jnp.dot(other_ref[rows, :], other, preferred_element_type=jnp.float32)
            target_ref[rows, :] = part.astype(jnp.bfloat16)


def mix_twice(half, own, other, points):
    return pl.pallas_call(
        mix_kernel,
        name="mix_twice",
        out_shape=jax.ShapeDtypeStruct(points.shape, jnp.bfloat16),
        in_specs=[pl.BlockSpec(memory_space=pltpu.SMEM)] + [pl.BlockSpec(memory_space=pltpu.VMEM)] * 3,
        out_specs=pl.BlockSpec(memory_space=pltpu.VMEM),
        scratch_shapes=[pltpu.VMEM(points.shape, jnp.bfloat16)] * 2,
        compiler_params=pltpu.CompilerParams(vmem_limit_bytes=24 * 2**20),
        cost_estimate=pl.CostEstimate(flops=1_100_000_000, bytes_accessed=4_000_000, transcendentals=0),
    )(half, own, other, points)


def spread_kernel(place_ref, *refs):
    *source_refs, out_ref, wide_ref = refs
    lane = lax.broadcasted_iota(jnp.int32, (SUBLANES, LANES), 1)
    row_blocks = FUNCS // BLOCK
    column_tiles = FUNCS // 2 // LANES

    def one_pair(index, carry):
        for pair in (2 * index, 2 * index + 1):
            columns = pl.ds(pl.multiple_of(pair * 2 * LANES, 2 * LANES), 2 * LANES)
            entries = jnp.concatenate([source_ref[:, columns] for source_ref in source_refs], 0)
            spread = jnp.dot(place_ref[...], entries, preferred_element_type=jnp.float32)
            for side in range(2):
                for tile in range(column_tiles):
                    for rows in range(row_blocks // SUBLANES):
                        group = [
                            spread[
                                (tile * 4 + step) * row_blocks + rows * SUBLANES:
                                (tile * 4 + step) * row_blocks + (rows + 1) * SUBLANES,
                                side * LANES:(side + 1) * LANES,
                            ]
                            for step in range(4)
                        ]
                        for fun, value in enumerate(swap_chunks(group, lane)):
                            start = tile * FUNCS + side * (FUNCS // 2)
                            start = start + rows * SUBLANES * (BLOCK // 2) + pair * FUN_DEV + fun
                            wide_ref[pl.ds(start, SUBLANES, stride=BLOCK // 2), :] = value
        return carry

    lax.fori_loop(0, BLOCK * BLOCK // 2 // (4 * LANES), one_pair, 0)
    for tile in range(column_tiles):
        out_ref[:, tile * LANES:(tile + 1) * LANES] = wide_ref[tile * FUNCS:(tile + 1) * FUNCS, :].astype(jnp.bfloat16)


def spread_blocks(place, *sources):
    return pl.pallas_call(
        spread_kernel,
        name="spread_blocks",
        out_shape=jax.ShapeDtypeStruct((FUNCS, FUNCS // 2), jnp.bfloat16),
        in_specs=[pl.BlockSpec(memory_space=pltpu.VMEM)] * (1 + len(sources)),
        out_specs=pl.BlockSpec(memory_space=pltpu.VMEM),
        scratch_shapes=[pltpu.VMEM((FUNCS * FUNCS // 2 // LANES, LANES), jnp.float32)],
        compiler_params=pltpu.CompilerParams(vmem_limit_bytes=60 * 2**20),
        cost_estimate=pl.CostEstimate(flops=200_000_000, bytes_accessed=8_000_000, transcendentals=0),
    )(place, *sources)


def dense_halves(core, own, near, far, block_cols):
    row_blocks, slots = block_cols.shape
    entry = jnp.arange(slots * row_blocks)
    place = jnp.arange(row_blocks * row_blocks)
    column = block_cols.T.reshape(-1)
    cut = column.shape[0] // 2
    swapped = jnp.where(core == 0, column, jnp.concatenate([column[cut:], column[:cut]]))

    def chosen(column):
        return (
            (column[None, :] == place[:, None] // row_blocks)
            & (entry[None, :] % row_blocks == place[:, None] % row_blocks)
        ).astype(jnp.bfloat16)

    def flat(blocks):
        return blocks[0].transpose(1, 0, 2).reshape(-1, BLOCK * BLOCK // 2)

    return spread_blocks(chosen(column), flat(own)), spread_blocks(chosen(swapped), flat(near), flat(far))


def other_half_pairs(wide, narrow):
    pairs = []
    for target in range(wide * narrow):
        rest, low = divmod(target, 2)
        rest, core = divmod(rest, 2)
        rest, z = divmod(rest, 8)
        x, high = divmod(rest, 2)
        y = (high * 2 + low + (1 if core == 0 else 3)) % 4
        pairs.append(((((x * 2 + y // 2) * 8 + z) * 2 + core) * 2 + y % 2, target))
    return pairs


def local(functions, potential, cheb_coef, block_cols, kernel_halves):
    devices = lax.axis_size("wide") * lax.axis_size("narrow")
    own = GRID // devices
    wide, narrow = lax.axis_size("wide"), lax.axis_size("narrow")
    core = lax.axis_index("wide") % 2
    slots = kernel_halves.shape[2] // 2
    part = lax.dynamic_slice_in_dim(kernel_halves, core * slots, slots, 2)
    near = lax.ppermute(part, ("wide", "narrow"), other_half_pairs(wide, narrow))
    rows = functions.reshape(FUN_DEV, TILES, LANES).transpose(1, 0, 2).reshape(TILES * FUN_DEV, LANES)
    filtered = filter_twice(rows, potential, cheb_coef)
    filtered, near = lax.optimization_barrier((filtered, near))
    far = lax.ppermute(near, "wide", [(index, index ^ 1) for index in range(wide)])
    mixers = dense_halves(core, kernel_halves, near, far, block_cols)
    outgoing = filtered.reshape(devices, own // LANES, FUN_DEV, LANES).transpose(0, 2, 1, 3)
    outgoing = outgoing.reshape(devices, FUN_DEV, own)
    points = lax.all_to_all(outgoing, ("narrow", "wide"), split_axis=0, concat_axis=0, tiled=True)
    half = lax.axis_index("narrow").reshape(1)
    mixed = mix_twice(half, *mixers, points.reshape(FUNCS, own))
    result = lax.all_to_all(
        mixed.reshape(devices, FUN_DEV, own), ("narrow", "wide"), split_axis=0, concat_axis=0, tiled=True
    )
    return result.transpose(1, 0, 2).reshape(FUN_DEV, GRID)


def solution(mesh):
    return jax.shard_map(
        local,
        mesh=mesh,
        in_specs=(P(("wide", "narrow"), None), P(), P(), P(), P("narrow", None, None, None)),
        out_specs=P(("wide", "narrow"), None),
        check_vma=False,
    )
```

```python
import jax
import jax.numpy as jnp
from jax import lax
from jax.experimental import pallas as pl
from jax.experimental.pallas import tpu as pltpu
from jax.sharding import PartitionSpec as P

FUN_DEV = 4
BOX_X = 64
BOX_Y = 32
BOX_Z = 32
BLOCK = 64
DEGREE = 8
UPDATES = 2
GRID = 65536
FUNCS = 1024
LANES = 128
SUBLANES = 8
X_FAR = 2
X_IN = 8
PARTS = 16
Y_OUT = BOX_Y * BOX_Z // LANES
TILES = GRID // LANES


def swap_chunks(group, lane):
    low = lane < 64
    even = (lane // 32) % 2 == 0
    upper, lower = [], []
    for first, second in ((group[0], group[2]), (group[1], group[3])):
        upper.append(jnp.where(low, first, pltpu.roll(second, 64, 1)))
        lower.append(jnp.where(low, pltpu.roll(first, 64, 1), second))
    out = []
    for first, second in (upper, lower):
        out.append(jnp.where(even, first, pltpu.roll(second, 32, 1)))
        out.append(jnp.where(even, pltpu.roll(first, 96, 1), second))
    return out


def point_order(size):
    first = lax.broadcasted_iota(jnp.int32, (size, size), 0)
    second = lax.broadcasted_iota(jnp.int32, (size, size), 1)
    column = first // 32 * 32 + first % 8 * 4 + first // 8 % 4
    return (second == column).astype(jnp.float32).astype(jnp.bfloat16)


def filter_kernel(
    coef_hbm,
    potential_hbm,
    in_hbm,
    out_ref,
    coef_ref,
    potential_ref,
    in_ref,
    plane_ref,
    turned_ref,
    shift_ref,
    field_ref,
    even_ref,
    odd_ref,
    semaphores,
):
    arrivals = [
        pltpu.make_async_copy(source, target, semaphores.at[index])
        for index, (source, target) in enumerate(
            ((potential_hbm, potential_ref), (in_hbm, in_ref), (coef_hbm, coef_ref))
        )
    ]
    for arrival in arrivals:
        arrival.start()
    lane = lax.broadcasted_iota(jnp.int32, (SUBLANES, LANES), 1)
    row = lax.broadcasted_iota(jnp.int32, (SUBLANES, LANES), 0)
    y_out = (lane // FUN_DEV) % Y_OUT
    order_z = point_order(LANES)
    first = lax.broadcasted_iota(jnp.int32, (LANES, LANES), 0)
    second = lax.broadcasted_iota(jnp.int32, (LANES, LANES), 1)
    unit = (first == second).astype(jnp.float32).astype(jnp.bfloat16)
    x_rows = Y_OUT * FUN_DEV

    arrivals[0].wait()
    for yo in range(Y_OUT):
        for xo in range(BOX_X // SUBLANES):
            shifted = 0.5 * (potential_ref[xo * SUBLANES:(xo + 1) * SUBLANES, yo * LANES:(yo + 1) * LANES] - 1.0)
            for fun in range(FUN_DEV):
                start = xo * SUBLANES * x_rows + yo * FUN_DEV + fun
                plane_ref[pl.ds(start, SUBLANES, stride=x_rows), :] = shifted

    def rows_of(far, xi, out):
        return pl.ds((far * 32 + out * X_IN + xi) * x_rows, x_rows)

    arrivals[1].wait()
    for xi in range(X_IN):
        blocks = [(far, out) for far in range(X_FAR) for out in range(4)]
        fields = jnp.concatenate([in_ref[rows_of(far, xi, out), :] for far, out in blocks], 0)
        fields = lax.dot_general(order_z, fields, (((1,), (1,)), ((), ())), preferred_element_type=jnp.float32)
        for far in range(X_FAR):
            field_ref[far, xi] = fields[:, far * LANES:(far + 1) * LANES].reshape(PARTS, SUBLANES, LANES)
            shifts = jnp.concatenate([plane_ref[rows_of(far, xi, out), :] for out in range(4)], 0)
            turned_ref[far] = shifts.T
            for part in range(PARTS):
                shift_ref[far, xi, part] = turned_ref[far, pl.ds(part // 4 * 32 + part % 4, SUBLANES, stride=4), :]

    def plane_step(before, at, after, target, coefficient, scale, last, start, far, xi):
        near = {(part // 4, part % 4): at[part] for part in range(PARTS)}
        for index in range(4):
            near[index, 4] = jnp.where(row < SUBLANES - 1, pltpu.roll(near[index, 0], SUBLANES - 1, 0), 0.0)
            near[index, -1] = jnp.where(row > 0, pltpu.roll(near[index, 3], 1, 0), 0.0)
            near[4, index] = jnp.where(y_out < Y_OUT - 1, pltpu.roll(near[0, index], LANES - FUN_DEV, 1), 0.0)
            near[-1, index] = jnp.where(y_out > 0, pltpu.roll(near[3, index], FUN_DEV, 1), 0.0)
        ahead = {}
        for yi in range(-1, 4):
            for zi in range(-1, 4):
                if (yi, zi) not in ((-1, 3), (3, -1)):
                    ahead[yi, zi] = near[yi, zi + 1] + near[yi + 1, zi]
        for part in range(PARTS):
            yi, zi = part // 4, part % 4
            total = before[part] + after[part] + (ahead[yi, zi] + ahead[yi - 1, zi - 1])
            applied = shift_ref[far, xi, part] * at[part] - 0.25 * total
            if scale is not None:
                applied = scale * applied
            value = coefficient * field_ref[far, xi, part] + applied
            if not start:
                value = value - target[far, xi, part]
            if last:
                field_ref[far, xi, part] = value
            else:
                target[far, xi, part] = value

    def stencil_step(source, target, coefficient, scale=None, last=False, start=False):
        def plane(far, xi):
            return [source[far, xi, part] for part in range(PARTS)]

        def below(far):
            own = [pltpu.roll(v, 32, 1) for v in plane(far, X_IN - 1)]
            if far == 0:
                return [jnp.where(lane < 32, 0.0, v) for v in own]
            return [jnp.where(lane < 32, pltpu.roll(v, 32, 1), w) for v, w in zip(plane(0, X_IN - 1), own)]

        def above(far):
            own = [pltpu.roll(v, 96, 1) for v in plane(far, 0)]
            if far == 1:
                return [jnp.where(lane >= 96, 0.0, v) for v in own]
            return [jnp.where(lane >= 96, pltpu.roll(v, 96, 1), w) for v, w in zip(plane(1, 0), own)]

        for far in range(X_FAR):
            before, at = below(far), plane(far, 0)
            for xi in range(X_IN):
                after = plane(far, xi + 1) if xi < X_IN - 1 else above(far)
                plane_step(before, at, after, target, coefficient, scale, last, start, far, xi)
                before, at = at, after

    def one_update(update, carry):
        stencil_step(field_ref, odd_ref, coef_ref[DEGREE - 1], scale=coef_ref[DEGREE], start=True)
        stencil_step(odd_ref, even_ref, coef_ref[DEGREE - 2] - coef_ref[DEGREE], start=True)

        def two_orders(pair, carry):
            order = DEGREE - 3 - 2 * pair
            stencil_step(even_ref, odd_ref, coef_ref[order])
            stencil_step(odd_ref, even_ref, coef_ref[order - 1])
            return carry

        lax.fori_loop(0, DEGREE // 2 - 2, two_orders, 0)
        stencil_step(even_ref, odd_ref, coef_ref[1])
        stencil_step(odd_ref, even_ref, coef_ref[0], scale=0.5, last=True)
        return carry

    arrivals[2].wait()
    lax.fori_loop(0, UPDATES, one_update, 0)

    for xi in range(X_IN):
        fields = field_ref[:, xi].reshape(X_FAR * LANES, LANES).astype(jnp.bfloat16)
        fields = lax.dot_general(unit, fields, (((1,), (1,)), ((), ())), preferred_element_type=jnp.float32)
        fields = fields.astype(jnp.bfloat16)
        for far in range(X_FAR):
            for out in range(4):
                rows = fields[out * x_rows:(out + 1) * x_rows, far * LANES:(far + 1) * LANES]
                out_ref[rows_of(far, xi, out), :] = rows


def filter_twice(rows, potential, coefficient):
    vectors = pltpu.VMEM((X_FAR, X_IN, PARTS, SUBLANES, LANES), jnp.float32)
    return pl.pallas_call(
        filter_kernel,
        name="filter_twice",
        out_shape=jax.ShapeDtypeStruct(rows.shape, jnp.bfloat16),
        in_specs=[pl.BlockSpec(memory_space=pltpu.HBM)] * 3,
        out_specs=pl.BlockSpec(memory_space=pltpu.VMEM),
        scratch_shapes=[
            pltpu.SMEM(coefficient.shape, jnp.float32),
            pltpu.VMEM(potential.shape, jnp.float32),
            pltpu.VMEM(rows.shape, jnp.bfloat16),
            pltpu.VMEM(rows.shape, jnp.float32),
            pltpu.VMEM((X_FAR, LANES, LANES), jnp.float32),
            vectors,
            vectors,
            vectors,
            vectors,
            pltpu.SemaphoreType.DMA((3,)),
        ],
        compiler_params=pltpu.CompilerParams(vmem_limit_bytes=60 * 2**20),
        cost_estimate=pl.CostEstimate(flops=60_000_000, bytes_accessed=40_000_000, transcendentals=0),
    )(coefficient, potential, rows)


def mix_kernel(half_ref, own_ref, other_ref, points_ref, out_ref, first_ref, middle_ref):
    size = points_ref.shape[1]
    points = jnp.dot(points_ref[...], point_order(size), preferred_element_type=jnp.float32)
    first_ref[...] = points.astype(jnp.bfloat16)
    count = FUNCS // 2
    for source_ref, target_ref in ((first_ref, middle_ref), (middle_ref, out_ref)):
        own = source_ref[pl.ds(pl.multiple_of(half_ref[0] * count, count), count), :]
        other = source_ref[pl.ds(pl.multiple_of((1 - half_ref[0]) * count, count), count), :]
        for start in range(0, FUNCS, size):
            rows = slice(start, start + size)
            part = jnp.dot(own_ref[rows, :], own, preferred_element_type=jnp.float32)
            part = part + jnp.dot(other_ref[rows, :], other, preferred_element_type=jnp.float32)
            target_ref[rows, :] = part.astype(jnp.bfloat16)


def mix_twice(half, own, other, points):
    return pl.pallas_call(
        mix_kernel,
        name="mix_twice",
        out_shape=jax.ShapeDtypeStruct(points.shape, jnp.bfloat16),
        in_specs=[pl.BlockSpec(memory_space=pltpu.SMEM)] + [pl.BlockSpec(memory_space=pltpu.VMEM)] * 3,
        out_specs=pl.BlockSpec(memory_space=pltpu.VMEM),
        scratch_shapes=[pltpu.VMEM(points.shape, jnp.bfloat16)] * 2,
        compiler_params=pltpu.CompilerParams(vmem_limit_bytes=24 * 2**20),
        cost_estimate=pl.CostEstimate(flops=1_100_000_000, bytes_accessed=4_000_000, transcendentals=0),
    )(half, own, other, points)


def spread_kernel(core_ref, place_ref, *refs):
    *source_refs, out_ref, wide_ref = refs
    lane = lax.broadcasted_iota(jnp.int32, (SUBLANES, LANES), 1)
    row_blocks = FUNCS // BLOCK
    column_tiles = FUNCS // 2 // LANES

    def one_pair(index, carry):
        for pair in (2 * index, 2 * index + 1):
            columns = pl.ds(pl.multiple_of(pair * 2 * LANES, 2 * LANES), 2 * LANES)
            parts = [source_ref[:, columns] for source_ref in source_refs]
            entries = jnp.concatenate(parts, 0)
            if len(parts) > 1:
                entries = jnp.where(core_ref[0] == 0, entries, jnp.concatenate(parts[::-1], 0))
            spread = jnp.dot(place_ref[...], entries, preferred_element_type=jnp.float32)
            for side in range(2):
                for tile in range(column_tiles):
                    for rows in range(row_blocks // SUBLANES):
                        group = [
                            spread[
                                (tile * 4 + step) * row_blocks + rows * SUBLANES:
                                (tile * 4 + step) * row_blocks + (rows + 1) * SUBLANES,
                                side * LANES:(side + 1) * LANES,
                            ]
                            for step in range(4)
                        ]
                        for fun, value in enumerate(swap_chunks(group, lane)):
                            start = tile * FUNCS + side * (FUNCS // 2)
                            start = start + rows * SUBLANES * (BLOCK // 2) + pair * FUN_DEV + fun
                            wide_ref[pl.ds(start, SUBLANES, stride=BLOCK // 2), :] = value
        return carry

    lax.fori_loop(0, BLOCK * BLOCK // 2 // (4 * LANES), one_pair, 0)
    for tile in range(column_tiles):
        out_ref[:, tile * LANES:(tile + 1) * LANES] = wide_ref[tile * FUNCS:(tile + 1) * FUNCS, :].astype(jnp.bfloat16)


def spread_blocks(vmem, core, place, *sources):
    return pl.pallas_call(
        spread_kernel,
        name="spread_blocks",
        out_shape=jax.ShapeDtypeStruct((FUNCS, FUNCS // 2), jnp.bfloat16),
        in_specs=[pl.BlockSpec(memory_space=pltpu.SMEM)] + [pl.BlockSpec(memory_space=pltpu.VMEM)] * (1 + len(sources)),
        out_specs=pl.BlockSpec(memory_space=pltpu.VMEM),
        scratch_shapes=[pltpu.VMEM((FUNCS * FUNCS // 2 // LANES, LANES), jnp.float32)],
        compiler_params=pltpu.CompilerParams(vmem_limit_bytes=vmem * 2**20),
        cost_estimate=pl.CostEstimate(flops=200_000_000, bytes_accessed=8_000_000, transcendentals=0),
    )(core, place, *sources)


def dense_halves(core, own, near, far, block_cols):
    row_blocks, slots = block_cols.shape
    entry = jnp.arange(slots * row_blocks)
    place = jnp.arange(row_blocks * row_blocks)
    column = block_cols.T.reshape(-1)
    chosen = (
        (column[None, :] == place[:, None] // row_blocks)
        & (entry[None, :] % row_blocks == place[:, None] % row_blocks)
    ).astype(jnp.bfloat16)

    def flat(blocks):
        return blocks[0].transpose(1, 0, 2).reshape(-1, BLOCK * BLOCK // 2)

    core = core.reshape(1)
    return spread_blocks(60, core, chosen, flat(own)), spread_blocks(16, core, chosen, flat(near), flat(far))


def other_half_pairs(wide, narrow):
    pairs = []
    for target in range(wide * narrow):
        rest, low = divmod(target, 2)
        rest, core = divmod(rest, 2)
        rest, z = divmod(rest, 8)
        x, high = divmod(rest, 2)
        y = (high * 2 + low + (1 if core == 0 else 3)) % 4
        pairs.append(((((x * 2 + y // 2) * 8 + z) * 2 + core) * 2 + y % 2, target))
    return pairs


def local(functions, potential, cheb_coef, block_cols, kernel_halves):
    devices = lax.axis_size("wide") * lax.axis_size("narrow")
    own = GRID // devices
    wide, narrow = lax.axis_size("wide"), lax.axis_size("narrow")
    core = lax.axis_index("wide") % 2
    slots = kernel_halves.shape[2] // 2
    part = lax.dynamic_slice_in_dim(kernel_halves, core * slots, slots, 2)
    near = lax.ppermute(part, ("wide", "narrow"), other_half_pairs(wide, narrow))
    rows = functions.reshape(FUN_DEV, TILES, LANES).transpose(1, 0, 2).reshape(TILES * FUN_DEV, LANES)
    filtered = filter_twice(rows, potential, cheb_coef)
    filtered, near = lax.optimization_barrier((filtered, near))
    far = lax.ppermute(near, "wide", [(index, index ^ 1) for index in range(wide)])
    mixers = dense_halves(core, kernel_halves, near, far, block_cols)
    outgoing = filtered.reshape(devices, own // LANES, FUN_DEV, LANES).transpose(0, 2, 1, 3)
    outgoing = outgoing.reshape(devices, FUN_DEV, own)
    points = lax.all_to_all(outgoing, ("narrow", "wide"), split_axis=0, concat_axis=0, tiled=True)
    half = lax.axis_index("narrow").reshape(1)
    mixed = mix_twice(half, *mixers, points.reshape(FUNCS, own))
    result = lax.all_to_all(
        mixed.reshape(devices, FUN_DEV, own), ("narrow", "wide"), split_axis=0, concat_axis=0, tiled=True
    )
    return result.transpose(1, 0, 2).reshape(FUN_DEV, GRID)


def solution(mesh):
    return jax.shard_map(
        local,
        mesh=mesh,
        in_specs=(P(("wide", "narrow"), None), P(), P(), P(), P("narrow", None, None, None)),
        out_specs=P(("wide", "narrow"), None),
        check_vma=False,
    )
```

```python
import jax
import jax.numpy as jnp
from jax import lax
from jax.experimental import pallas as pl
from jax.experimental.pallas import tpu as pltpu
from jax.sharding import PartitionSpec as P

FUN_DEV = 4
BOX_X = 64
BOX_Y = 32
BOX_Z = 32
BLOCK = 64
DEGREE = 8
UPDATES = 2
GRID = 65536
FUNCS = 1024
LANES = 128
SUBLANES = 8
X_FAR = 2
X_IN = 8
PARTS = 16
Y_OUT = BOX_Y * BOX_Z // LANES
TILES = GRID // LANES


def swap_chunks(group, lane):
    low = lane < 64
    even = (lane // 32) % 2 == 0
    upper, lower = [], []
    for first, second in ((group[0], group[2]), (group[1], group[3])):
        upper.append(jnp.where(low, first, pltpu.roll(second, 64, 1)))
        lower.append(jnp.where(low, pltpu.roll(first, 64, 1), second))
    out = []
    for first, second in (upper, lower):
        out.append(jnp.where(even, first, pltpu.roll(second, 32, 1)))
        out.append(jnp.where(even, pltpu.roll(first, 96, 1), second))
    return out


def point_order(size):
    first = lax.broadcasted_iota(jnp.int32, (size, size), 0)
    second = lax.broadcasted_iota(jnp.int32, (size, size), 1)
    column = first // 32 * 32 + first % 8 * 4 + first // 8 % 4
    return (second == column).astype(jnp.float32).astype(jnp.bfloat16)


def filter_kernel(
    coef_hbm,
    potential_hbm,
    in_hbm,
    out_ref,
    coef_ref,
    potential_ref,
    in_ref,
    plane_ref,
    turned_ref,
    shift_ref,
    field_ref,
    even_ref,
    odd_ref,
    semaphores,
):
    arrivals = [
        pltpu.make_async_copy(source, target, semaphores.at[index])
        for index, (source, target) in enumerate(
            ((potential_hbm, potential_ref), (in_hbm, in_ref), (coef_hbm, coef_ref))
        )
    ]
    for arrival in arrivals:
        arrival.start()
    lane = lax.broadcasted_iota(jnp.int32, (SUBLANES, LANES), 1)
    row = lax.broadcasted_iota(jnp.int32, (SUBLANES, LANES), 0)
    y_out = (lane // FUN_DEV) % Y_OUT
    order_z = point_order(LANES)
    first = lax.broadcasted_iota(jnp.int32, (LANES, LANES), 0)
    second = lax.broadcasted_iota(jnp.int32, (LANES, LANES), 1)
    unit = (first == second).astype(jnp.float32).astype(jnp.bfloat16)
    x_rows = Y_OUT * FUN_DEV

    arrivals[0].wait()
    for yo in range(Y_OUT):
        for xo in range(BOX_X // SUBLANES):
            shifted = 0.5 * (potential_ref[xo * SUBLANES:(xo + 1) * SUBLANES, yo * LANES:(yo + 1) * LANES] - 1.0)
            for fun in range(FUN_DEV):
                start = xo * SUBLANES * x_rows + yo * FUN_DEV + fun
                plane_ref[pl.ds(start, SUBLANES, stride=x_rows), :] = shifted

    def rows_of(far, xi, out):
        return pl.ds((far * 32 + out * X_IN + xi) * x_rows, x_rows)

    arrivals[1].wait()
    for xi in range(X_IN):
        blocks = [(far, out) for far in range(X_FAR) for out in range(4)]
        fields = jnp.concatenate([in_ref[rows_of(far, xi, out), :] for far, out in blocks], 0)
        fields = lax.dot_general(order_z, fields, (((1,), (1,)), ((), ())), preferred_element_type=jnp.float32)
        for far in range(X_FAR):
            field_ref[far, xi] = fields[:, far * LANES:(far + 1) * LANES].reshape(PARTS, SUBLANES, LANES)
            shifts = jnp.concatenate([plane_ref[rows_of(far, xi, out), :] for out in range(4)], 0)
            turned_ref[far] = shifts.T
            for part in range(PARTS):
                shift_ref[far, xi, part] = turned_ref[far, pl.ds(part // 4 * 32 + part % 4, SUBLANES, stride=4), :]

    def plane_step(before, at, after, target, coefficient, scale, last, start, far, xi):
        near = {(part // 4, part % 4): at[part] for part in range(PARTS)}
        for index in range(4):
            near[index, 4] = jnp.where(row < SUBLANES - 1, pltpu.roll(near[index, 0], SUBLANES - 1, 0), 0.0)
            near[index, -1] = jnp.where(row > 0, pltpu.roll(near[index, 3], 1, 0), 0.0)
            near[4, index] = jnp.where(y_out < Y_OUT - 1, pltpu.roll(near[0, index], LANES - FUN_DEV, 1), 0.0)
            near[-1, index] = jnp.where(y_out > 0, pltpu.roll(near[3, index], FUN_DEV, 1), 0.0)
        ahead = {}
        for yi in range(-1, 4):
            for zi in range(-1, 4):
                if (yi, zi) not in ((-1, 3), (3, -1)):
                    ahead[yi, zi] = near[yi, zi + 1] + near[yi + 1, zi]
        for part in range(PARTS):
            yi, zi = part // 4, part % 4
            total = before[part] + after[part] + (ahead[yi, zi] + ahead[yi - 1, zi - 1])
            applied = shift_ref[far, xi, part] * at[part] - 0.25 * total
            if scale is not None:
                applied = scale * applied
            value = coefficient * field_ref[far, xi, part] + applied
            if not start:
                value = value - target[far, xi, part]
            if last:
                field_ref[far, xi, part] = value
            else:
                target[far, xi, part] = value

    def stencil_step(source, target, coefficient, scale=None, last=False, start=False):
        def plane(far, xi):
            return [source[far, xi, part] for part in range(PARTS)]

        def below(far):
            own = [pltpu.roll(v, 32, 1) for v in plane(far, X_IN - 1)]
            if far == 0:
                return [jnp.where(lane < 32, 0.0, v) for v in own]
            return [jnp.where(lane < 32, pltpu.roll(v, 32, 1), w) for v, w in zip(plane(0, X_IN - 1), own)]

        def above(far):
            own = [pltpu.roll(v, 96, 1) for v in plane(far, 0)]
            if far == 1:
                return [jnp.where(lane >= 96, 0.0, v) for v in own]
            return [jnp.where(lane >= 96, pltpu.roll(v, 96, 1), w) for v, w in zip(plane(1, 0), own)]

        for far in range(X_FAR):
            before, at = below(far), plane(far, 0)
            for xi in range(X_IN):
                after = plane(far, xi + 1) if xi < X_IN - 1 else above(far)
                plane_step(before, at, after, target, coefficient, scale, last, start, far, xi)
                before, at = at, after

    def one_update(update, carry):
        stencil_step(field_ref, odd_ref, coef_ref[DEGREE - 1], scale=coef_ref[DEGREE], start=True)
        stencil_step(odd_ref, even_ref, coef_ref[DEGREE - 2] - coef_ref[DEGREE], start=True)

        def two_orders(pair, carry):
            order = DEGREE - 3 - 2 * pair
            stencil_step(even_ref, odd_ref, coef_ref[order])
            stencil_step(odd_ref, even_ref, coef_ref[order - 1])
            return carry

        lax.fori_loop(0, DEGREE // 2 - 2, two_orders, 0)
        stencil_step(even_ref, odd_ref, coef_ref[1])
        stencil_step(odd_ref, even_ref, coef_ref[0], scale=0.5, last=True)
        return carry

    arrivals[2].wait()
    lax.fori_loop(0, UPDATES, one_update, 0)

    for xi in range(X_IN):
        fields = field_ref[:, xi].reshape(X_FAR * LANES, LANES).astype(jnp.bfloat16)
        fields = lax.dot_general(unit, fields, (((1,), (1,)), ((), ())), preferred_element_type=jnp.float32)
        fields = fields.astype(jnp.bfloat16)
        for far in range(X_FAR):
            for out in range(4):
                rows = fields[out * x_rows:(out + 1) * x_rows, far * LANES:(far + 1) * LANES]
                out_ref[rows_of(far, xi, out), :] = rows


def filter_twice(rows, potential, coefficient):
    vectors = pltpu.VMEM((X_FAR, X_IN, PARTS, SUBLANES, LANES), jnp.float32)
    return pl.pallas_call(
        filter_kernel,
        name="filter_twice",
        out_shape=jax.ShapeDtypeStruct(rows.shape, jnp.bfloat16),
        in_specs=[pl.BlockSpec(memory_space=pltpu.HBM)] * 3,
        out_specs=pl.BlockSpec(memory_space=pltpu.VMEM),
        scratch_shapes=[
            pltpu.SMEM(coefficient.shape, jnp.float32),
            pltpu.VMEM(potential.shape, jnp.float32),
            pltpu.VMEM(rows.shape, jnp.bfloat16),
            pltpu.VMEM(rows.shape, jnp.float32),
            pltpu.VMEM((X_FAR, LANES, LANES), jnp.float32),
            vectors,
            vectors,
            vectors,
            vectors,
            pltpu.SemaphoreType.DMA((3,)),
        ],
        compiler_params=pltpu.CompilerParams(vmem_limit_bytes=60 * 2**20),
        cost_estimate=pl.CostEstimate(flops=60_000_000, bytes_accessed=40_000_000, transcendentals=0),
    )(coefficient, potential, rows)


def mix_kernel(half_ref, own_ref, other_ref, points_ref, out_ref, first_ref, middle_ref):
    size = points_ref.shape[1]
    points = jnp.dot(points_ref[...], point_order(size), preferred_element_type=jnp.float32)
    first_ref[...] = points.astype(jnp.bfloat16)
    count = FUNCS // 2
    for source_ref, target_ref in ((first_ref, middle_ref), (middle_ref, out_ref)):
        own = source_ref[pl.ds(pl.multiple_of(half_ref[0] * count, count), count), :]
        other = source_ref[pl.ds(pl.multiple_of((1 - half_ref[0]) * count, count), count), :]
        for start in range(0, FUNCS, size):
            rows = slice(start, start + size)
            part = jnp.dot(own_ref[rows, :], own, preferred_element_type=jnp.float32)
            part = part + jnp.dot(other_ref[rows, :], other, preferred_element_type=jnp.float32)
            target_ref[rows, :] = part.astype(jnp.bfloat16)


def mix_twice(half, own, other, points):
    return pl.pallas_call(
        mix_kernel,
        name="mix_twice",
        out_shape=jax.ShapeDtypeStruct(points.shape, jnp.bfloat16),
        in_specs=[pl.BlockSpec(memory_space=pltpu.SMEM)] + [pl.BlockSpec(memory_space=pltpu.VMEM)] * 3,
        out_specs=pl.BlockSpec(memory_space=pltpu.VMEM),
        scratch_shapes=[pltpu.VMEM(points.shape, jnp.bfloat16)] * 2,
        compiler_params=pltpu.CompilerParams(vmem_limit_bytes=24 * 2**20),
        cost_estimate=pl.CostEstimate(flops=1_100_000_000, bytes_accessed=4_000_000, transcendentals=0),
    )(half, own, other, points)


def spread_kernel(core_ref, place_ref, *refs):
    *source_refs, out_ref, wide_ref = refs
    lane = lax.broadcasted_iota(jnp.int32, (SUBLANES, LANES), 1)
    row_blocks = FUNCS // BLOCK
    column_tiles = FUNCS // 2 // LANES

    def one_pair(index, carry):
        for pair in (2 * index, 2 * index + 1):
            columns = pl.ds(pl.multiple_of(pair * 2 * LANES, 2 * LANES), 2 * LANES)
            parts = [source_ref[:, columns] for source_ref in source_refs]
            entries = jnp.concatenate(parts, 0)
            if len(parts) > 1:
                entries = jnp.where(core_ref[0] == 0, entries, jnp.concatenate(parts[::-1], 0))
            spread = jnp.dot(place_ref[...], entries, preferred_element_type=jnp.float32)
            for side in range(2):
                for tile in range(column_tiles):
                    for rows in range(row_blocks // SUBLANES):
                        group = [
                            spread[
                                (tile * 4 + step) * row_blocks + rows * SUBLANES:
                                (tile * 4 + step) * row_blocks + (rows + 1) * SUBLANES,
                                side * LANES:(side + 1) * LANES,
                            ]
                            for step in range(4)
                        ]
                        for fun, value in enumerate(swap_chunks(group, lane)):
                            start = tile * FUNCS + side * (FUNCS // 2)
                            start = start + rows * SUBLANES * (BLOCK // 2) + pair * FUN_DEV + fun
                            wide_ref[pl.ds(start, SUBLANES, stride=BLOCK // 2), :] = value
        return carry

    lax.fori_loop(0, BLOCK * BLOCK // 2 // (4 * LANES), one_pair, 0)
    for tile in range(column_tiles):
        out_ref[:, tile * LANES:(tile + 1) * LANES] = wide_ref[tile * FUNCS:(tile + 1) * FUNCS, :].astype(jnp.bfloat16)


def spread_blocks(vmem, core, place, *sources):
    return pl.pallas_call(
        spread_kernel,
        name="spread_blocks",
        out_shape=jax.ShapeDtypeStruct((FUNCS, FUNCS // 2), jnp.bfloat16),
        in_specs=[pl.BlockSpec(memory_space=pltpu.SMEM)] + [pl.BlockSpec(memory_space=pltpu.VMEM)] * (1 + len(sources)),
        out_specs=pl.BlockSpec(memory_space=pltpu.VMEM),
        scratch_shapes=[pltpu.VMEM((FUNCS * FUNCS // 2 // LANES, LANES), jnp.float32)],
        compiler_params=pltpu.CompilerParams(vmem_limit_bytes=vmem * 2**20),
        cost_estimate=pl.CostEstimate(flops=200_000_000, bytes_accessed=8_000_000, transcendentals=0),
    )(core, place, *sources)


def dense_halves(core, own, near, swap, block_cols):
    row_blocks, slots = block_cols.shape
    entry = jnp.arange(slots * row_blocks)
    place = jnp.arange(row_blocks * row_blocks)
    column = block_cols.T.reshape(-1)
    chosen = (
        (column[None, :] == place[:, None] // row_blocks)
        & (entry[None, :] % row_blocks == place[:, None] % row_blocks)
    ).astype(jnp.bfloat16)

    def flat(blocks):
        return blocks[0].transpose(1, 0, 2).reshape(-1, BLOCK * BLOCK // 2)

    core = core.reshape(1)
    own, near = lax.optimization_barrier((spread_blocks(60, core, chosen, flat(own)), near))
    far = lax.ppermute(near, "wide", swap)
    return own, spread_blocks(16, core, chosen, flat(near), flat(far))


def other_half_pairs(wide, narrow):
    pairs = []
    for target in range(wide * narrow):
        rest, low = divmod(target, 2)
        rest, core = divmod(rest, 2)
        rest, z = divmod(rest, 8)
        x, high = divmod(rest, 2)
        y = (high * 2 + low + (1 if core == 0 else 3)) % 4
        pairs.append(((((x * 2 + y // 2) * 8 + z) * 2 + core) * 2 + y % 2, target))
    return pairs


def local(functions, potential, cheb_coef, block_cols, kernel_halves):
    devices = lax.axis_size("wide") * lax.axis_size("narrow")
    own = GRID // devices
    wide, narrow = lax.axis_size("wide"), lax.axis_size("narrow")
    core = lax.axis_index("wide") % 2
    slots = kernel_halves.shape[2] // 2
    part = lax.dynamic_slice_in_dim(kernel_halves, core * slots, slots, 2)
    near = lax.ppermute(part, ("wide", "narrow"), other_half_pairs(wide, narrow))
    rows = functions.reshape(FUN_DEV, TILES, LANES).transpose(1, 0, 2).reshape(TILES * FUN_DEV, LANES)
    filtered = filter_twice(rows, potential, cheb_coef)
    swap = [(index, index ^ 1) for index in range(wide)]
    mixers = dense_halves(core, kernel_halves, near, swap, block_cols)
    outgoing = filtered.reshape(devices, own // LANES, FUN_DEV, LANES).transpose(0, 2, 1, 3)
    outgoing = outgoing.reshape(devices, FUN_DEV, own)
    points = lax.all_to_all(outgoing, ("narrow", "wide"), split_axis=0, concat_axis=0, tiled=True)
    half = lax.axis_index("narrow").reshape(1)
    mixed = mix_twice(half, *mixers, points.reshape(FUNCS, own))
    result = lax.all_to_all(
        mixed.reshape(devices, FUN_DEV, own), ("narrow", "wide"), split_axis=0, concat_axis=0, tiled=True
    )
    return result.transpose(1, 0, 2).reshape(FUN_DEV, GRID)


def solution(mesh):
    return jax.shard_map(
        local,
        mesh=mesh,
        in_specs=(P(("wide", "narrow"), None), P(), P(), P(), P("narrow", None, None, None)),
        out_specs=P(("wide", "narrow"), None),
        check_vma=False,
    )
```

```python
import jax
import jax.numpy as jnp
from jax import lax
from jax.experimental import pallas as pl
from jax.experimental.pallas import tpu as pltpu
from jax.sharding import PartitionSpec as P

FUN_DEV = 4
BOX_X = 64
BOX_Y = 32
BOX_Z = 32
BLOCK = 64
DEGREE = 8
UPDATES = 2
GRID = 65536
FUNCS = 1024
LANES = 128
SUBLANES = 8
X_FAR = 2
X_IN = 8
PARTS = 16
Y_OUT = BOX_Y * BOX_Z // LANES
TILES = GRID // LANES


def swap_chunks(group, lane):
    low = lane < 64
    even = (lane // 32) % 2 == 0
    upper, lower = [], []
    for first, second in ((group[0], group[2]), (group[1], group[3])):
        upper.append(jnp.where(low, first, pltpu.roll(second, 64, 1)))
        lower.append(jnp.where(low, pltpu.roll(first, 64, 1), second))
    out = []
    for first, second in (upper, lower):
        out.append(jnp.where(even, first, pltpu.roll(second, 32, 1)))
        out.append(jnp.where(even, pltpu.roll(first, 96, 1), second))
    return out


def point_order(size):
    first = lax.broadcasted_iota(jnp.int32, (size, size), 0)
    second = lax.broadcasted_iota(jnp.int32, (size, size), 1)
    column = first // 32 * 32 + first % 8 * 4 + first // 8 % 4
    return (second == column).astype(jnp.float32).astype(jnp.bfloat16)


def filter_kernel(
    coef_hbm,
    potential_hbm,
    in_hbm,
    out_ref,
    coef_ref,
    potential_ref,
    in_ref,
    plane_ref,
    turned_ref,
    shift_ref,
    field_ref,
    even_ref,
    odd_ref,
    semaphores,
):
    arrivals = [
        pltpu.make_async_copy(source, target, semaphores.at[index])
        for index, (source, target) in enumerate(
            ((potential_hbm, potential_ref), (in_hbm, in_ref), (coef_hbm, coef_ref))
        )
    ]
    for arrival in arrivals:
        arrival.start()
    lane = lax.broadcasted_iota(jnp.int32, (SUBLANES, LANES), 1)
    row = lax.broadcasted_iota(jnp.int32, (SUBLANES, LANES), 0)
    y_out = (lane // FUN_DEV) % Y_OUT
    order_z = point_order(LANES)
    first = lax.broadcasted_iota(jnp.int32, (LANES, LANES), 0)
    second = lax.broadcasted_iota(jnp.int32, (LANES, LANES), 1)
    unit = (first == second).astype(jnp.float32).astype(jnp.bfloat16)
    x_rows = Y_OUT * FUN_DEV

    arrivals[0].wait()
    for yo in range(Y_OUT):
        for xo in range(BOX_X // SUBLANES):
            shifted = 0.5 * (potential_ref[xo * SUBLANES:(xo + 1) * SUBLANES, yo * LANES:(yo + 1) * LANES] - 1.0)
            for fun in range(FUN_DEV):
                start = xo * SUBLANES * x_rows + yo * FUN_DEV + fun
                plane_ref[pl.ds(start, SUBLANES, stride=x_rows), :] = shifted

    def rows_of(far, xi, out):
        return pl.ds((far * 32 + out * X_IN + xi) * x_rows, x_rows)

    arrivals[1].wait()
    for xi in range(X_IN):
        blocks = [(far, out) for far in range(X_FAR) for out in range(4)]
        fields = jnp.concatenate([in_ref[rows_of(far, xi, out), :] for far, out in blocks], 0)
        fields = lax.dot_general(order_z, fields, (((1,), (1,)), ((), ())), preferred_element_type=jnp.float32)
        for far in range(X_FAR):
            field_ref[far, xi] = fields[:, far * LANES:(far + 1) * LANES].reshape(PARTS, SUBLANES, LANES)
            shifts = jnp.concatenate([plane_ref[rows_of(far, xi, out), :] for out in range(4)], 0)
            turned_ref[far] = shifts.T
            for part in range(PARTS):
                shift_ref[far, xi, part] = turned_ref[far, pl.ds(part // 4 * 32 + part % 4, SUBLANES, stride=4), :]

    def plane_step(before, at, after, target, coefficient, scale, last, start, far, xi):
        near = {(part // 4, part % 4): at[part] for part in range(PARTS)}
        for index in range(4):
            near[index, 4] = jnp.where(row < SUBLANES - 1, pltpu.roll(near[index, 0], SUBLANES - 1, 0), 0.0)
            near[index, -1] = jnp.where(row > 0, pltpu.roll(near[index, 3], 1, 0), 0.0)
            near[4, index] = jnp.where(y_out < Y_OUT - 1, pltpu.roll(near[0, index], LANES - FUN_DEV, 1), 0.0)
            near[-1, index] = jnp.where(y_out > 0, pltpu.roll(near[3, index], FUN_DEV, 1), 0.0)
        ahead = {}
        for yi in range(-1, 4):
            for zi in range(-1, 4):
                if (yi, zi) not in ((-1, 3), (3, -1)):
                    ahead[yi, zi] = near[yi, zi + 1] + near[yi + 1, zi]
        for part in range(PARTS):
            yi, zi = part // 4, part % 4
            total = before[part] + after[part] + (ahead[yi, zi] + ahead[yi - 1, zi - 1])
            applied = shift_ref[far, xi, part] * at[part] - 0.25 * total
            if scale is not None:
                applied = scale * applied
            value = coefficient * field_ref[far, xi, part] + applied
            if not start:
                value = value - target[far, xi, part]
            if last:
                field_ref[far, xi, part] = value
            else:
                target[far, xi, part] = value

    def stencil_step(source, target, coefficient, scale=None, last=False, start=False):
        def plane(far, xi):
            return [source[far, xi, part] for part in range(PARTS)]

        def below(far):
            own = [pltpu.roll(v, 32, 1) for v in plane(far, X_IN - 1)]
            if far == 0:
                return [jnp.where(lane < 32, 0.0, v) for v in own]
            return [jnp.where(lane < 32, pltpu.roll(v, 32, 1), w) for v, w in zip(plane(0, X_IN - 1), own)]

        def above(far):
            own = [pltpu.roll(v, 96, 1) for v in plane(far, 0)]
            if far == 1:
                return [jnp.where(lane >= 96, 0.0, v) for v in own]
            return [jnp.where(lane >= 96, pltpu.roll(v, 96, 1), w) for v, w in zip(plane(1, 0), own)]

        for far in range(X_FAR):
            before, at = below(far), plane(far, 0)
            for xi in range(X_IN):
                after = plane(far, xi + 1) if xi < X_IN - 1 else above(far)
                plane_step(before, at, after, target, coefficient, scale, last, start, far, xi)
                before, at = at, after

    def one_update(update, carry):
        stencil_step(field_ref, odd_ref, coef_ref[DEGREE - 1], scale=coef_ref[DEGREE], start=True)
        stencil_step(odd_ref, even_ref, coef_ref[DEGREE - 2] - coef_ref[DEGREE], start=True)

        def two_orders(pair, carry):
            order = DEGREE - 3 - 2 * pair
            stencil_step(even_ref, odd_ref, coef_ref[order])
            stencil_step(odd_ref, even_ref, coef_ref[order - 1])
            return carry

        lax.fori_loop(0, DEGREE // 2 - 2, two_orders, 0)
        stencil_step(even_ref, odd_ref, coef_ref[1])
        stencil_step(odd_ref, even_ref, coef_ref[0], scale=0.5, last=True)
        return carry

    arrivals[2].wait()
    lax.fori_loop(0, UPDATES, one_update, 0)

    for xi in range(X_IN):
        fields = field_ref[:, xi].reshape(X_FAR * LANES, LANES).astype(jnp.bfloat16)
        fields = lax.dot_general(unit, fields, (((1,), (1,)), ((), ())), preferred_element_type=jnp.float32)
        fields = fields.astype(jnp.bfloat16)
        for far in range(X_FAR):
            for out in range(4):
                rows = fields[out * x_rows:(out + 1) * x_rows, far * LANES:(far + 1) * LANES]
                out_ref[rows_of(far, xi, out), :] = rows


def filter_twice(rows, potential, coefficient):
    vectors = pltpu.VMEM((X_FAR, X_IN, PARTS, SUBLANES, LANES), jnp.float32)
    return pl.pallas_call(
        filter_kernel,
        name="filter_twice",
        out_shape=jax.ShapeDtypeStruct(rows.shape, jnp.bfloat16),
        in_specs=[pl.BlockSpec(memory_space=pltpu.HBM)] * 3,
        out_specs=pl.BlockSpec(memory_space=pltpu.VMEM),
        scratch_shapes=[
            pltpu.SMEM(coefficient.shape, jnp.float32),
            pltpu.VMEM(potential.shape, jnp.float32),
            pltpu.VMEM(rows.shape, jnp.bfloat16),
            pltpu.VMEM(rows.shape, jnp.float32),
            pltpu.VMEM((X_FAR, LANES, LANES), jnp.float32),
            vectors,
            vectors,
            vectors,
            vectors,
            pltpu.SemaphoreType.DMA((3,)),
        ],
        compiler_params=pltpu.CompilerParams(vmem_limit_bytes=60 * 2**20),
        cost_estimate=pl.CostEstimate(flops=60_000_000, bytes_accessed=40_000_000, transcendentals=0),
    )(coefficient, potential, rows)


def mix_kernel(half_ref, own_ref, other_ref, points_ref, out_ref, first_ref, middle_ref):
    size = points_ref.shape[1]
    points = jnp.dot(points_ref[...], point_order(size), preferred_element_type=jnp.float32)
    first_ref[...] = points.astype(jnp.bfloat16)
    count = FUNCS // 2
    for source_ref, target_ref in ((first_ref, middle_ref), (middle_ref, out_ref)):
        own = source_ref[pl.ds(pl.multiple_of(half_ref[0] * count, count), count), :]
        other = source_ref[pl.ds(pl.multiple_of((1 - half_ref[0]) * count, count), count), :]
        both = jnp.concatenate([own, other], 0)
        for start in range(0, FUNCS, size):
            rows = slice(start, start + size)
            mixer = jnp.concatenate([own_ref[rows, :], other_ref[rows, :]], 1)
            part = jnp.dot(mixer, both, preferred_element_type=jnp.float32)
            target_ref[rows, :] = part.astype(jnp.bfloat16)


def mix_twice(half, own, other, points):
    return pl.pallas_call(
        mix_kernel,
        name="mix_twice",
        out_shape=jax.ShapeDtypeStruct(points.shape, jnp.bfloat16),
        in_specs=[pl.BlockSpec(memory_space=pltpu.SMEM)] + [pl.BlockSpec(memory_space=pltpu.VMEM)] * 3,
        out_specs=pl.BlockSpec(memory_space=pltpu.VMEM),
        scratch_shapes=[pltpu.VMEM(points.shape, jnp.bfloat16)] * 2,
        compiler_params=pltpu.CompilerParams(vmem_limit_bytes=24 * 2**20),
        cost_estimate=pl.CostEstimate(flops=1_100_000_000, bytes_accessed=4_000_000, transcendentals=0),
    )(half, own, other, points)


def spread_kernel(core_ref, place_ref, *refs):
    *source_refs, out_ref, wide_ref = refs
    lane = lax.broadcasted_iota(jnp.int32, (SUBLANES, LANES), 1)
    row_blocks = FUNCS // BLOCK
    column_tiles = FUNCS // 2 // LANES

    def one_pair(index, carry):
        for pair in (2 * index, 2 * index + 1):
            columns = pl.ds(pl.multiple_of(pair * 2 * LANES, 2 * LANES), 2 * LANES)
            parts = [source_ref[:, columns] for source_ref in source_refs]
            entries = jnp.concatenate(parts, 0)
            if len(parts) > 1:
                entries = jnp.where(core_ref[0] == 0, entries, jnp.concatenate(parts[::-1], 0))
            spread = jnp.dot(place_ref[...], entries, preferred_element_type=jnp.float32)
            for side in range(2):
                for tile in range(column_tiles):
                    for rows in range(row_blocks // SUBLANES):
                        group = [
                            spread[
                                (tile * 4 + step) * row_blocks + rows * SUBLANES:
                                (tile * 4 + step) * row_blocks + (rows + 1) * SUBLANES,
                                side * LANES:(side + 1) * LANES,
                            ]
                            for step in range(4)
                        ]
                        for fun, value in enumerate(swap_chunks(group, lane)):
                            start = tile * FUNCS + side * (FUNCS // 2)
                            start = start + rows * SUBLANES * (BLOCK // 2) + pair * FUN_DEV + fun
                            wide_ref[pl.ds(start, SUBLANES, stride=BLOCK // 2), :] = value
        return carry

    lax.fori_loop(0, BLOCK * BLOCK // 2 // (4 * LANES), one_pair, 0)
    for tile in range(column_tiles):
        out_ref[:, tile * LANES:(tile + 1) * LANES] = wide_ref[tile * FUNCS:(tile + 1) * FUNCS, :].astype(jnp.bfloat16)


def spread_blocks(vmem, core, place, *sources):
    return pl.pallas_call(
        spread_kernel,
        name="spread_blocks",
        out_shape=jax.ShapeDtypeStruct((FUNCS, FUNCS // 2), jnp.bfloat16),
        in_specs=[pl.BlockSpec(memory_space=pltpu.SMEM)] + [pl.BlockSpec(memory_space=pltpu.VMEM)] * (1 + len(sources)),
        out_specs=pl.BlockSpec(memory_space=pltpu.VMEM),
        scratch_shapes=[pltpu.VMEM((FUNCS * FUNCS // 2 // LANES, LANES), jnp.float32)],
        compiler_params=pltpu.CompilerParams(vmem_limit_bytes=vmem * 2**20),
        cost_estimate=pl.CostEstimate(flops=200_000_000, bytes_accessed=8_000_000, transcendentals=0),
    )(core, place, *sources)


def dense_halves(core, own, near, far, block_cols):
    row_blocks, slots = block_cols.shape
    entry = jnp.arange(slots * row_blocks)
    place = jnp.arange(row_blocks * row_blocks)
    column = block_cols.T.reshape(-1)
    chosen = (
        (column[None, :] == place[:, None] // row_blocks)
        & (entry[None, :] % row_blocks == place[:, None] % row_blocks)
    ).astype(jnp.bfloat16)

    def flat(blocks):
        return blocks[0].transpose(1, 0, 2).reshape(-1, BLOCK * BLOCK // 2)

    core = core.reshape(1)
    return spread_blocks(60, core, chosen, flat(own)), spread_blocks(16, core, chosen, flat(near), flat(far))


def other_half_pairs(wide, narrow):
    pairs = []
    for target in range(wide * narrow):
        rest, low = divmod(target, 2)
        rest, core = divmod(rest, 2)
        rest, z = divmod(rest, 8)
        x, high = divmod(rest, 2)
        y = (high * 2 + low + (1 if core == 0 else 3)) % 4
        pairs.append(((((x * 2 + y // 2) * 8 + z) * 2 + core) * 2 + y % 2, target))
    return pairs


def local(functions, potential, cheb_coef, block_cols, kernel_halves):
    devices = lax.axis_size("wide") * lax.axis_size("narrow")
    own = GRID // devices
    wide, narrow = lax.axis_size("wide"), lax.axis_size("narrow")
    core = lax.axis_index("wide") % 2
    slots = kernel_halves.shape[2] // 2
    part = lax.dynamic_slice_in_dim(kernel_halves, core * slots, slots, 2)
    near = lax.ppermute(part, ("wide", "narrow"), other_half_pairs(wide, narrow))
    rows = functions.reshape(FUN_DEV, TILES, LANES).transpose(1, 0, 2).reshape(TILES * FUN_DEV, LANES)
    filtered = filter_twice(rows, potential, cheb_coef)
    filtered, near = lax.optimization_barrier((filtered, near))
    far = lax.ppermute(near, "wide", [(index, index ^ 1) for index in range(wide)])
    mixers = dense_halves(core, kernel_halves, near, far, block_cols)
    outgoing = filtered.reshape(devices, own // LANES, FUN_DEV, LANES).transpose(0, 2, 1, 3)
    outgoing = outgoing.reshape(devices, FUN_DEV, own)
    points = lax.all_to_all(outgoing, ("narrow", "wide"), split_axis=0, concat_axis=0, tiled=True)
    half = lax.axis_index("narrow").reshape(1)
    mixed = mix_twice(half, *mixers, points.reshape(FUNCS, own))
    result = lax.all_to_all(
        mixed.reshape(devices, FUN_DEV, own), ("narrow", "wide"), split_axis=0, concat_axis=0, tiled=True
    )
    return result.transpose(1, 0, 2).reshape(FUN_DEV, GRID)


def solution(mesh):
    return jax.shard_map(
        local,
        mesh=mesh,
        in_specs=(P(("wide", "narrow"), None), P(), P(), P(), P("narrow", None, None, None)),
        out_specs=P(("wide", "narrow"), None),
        check_vma=False,
    )
```
